32 devices in a mesh: blk: 8 (over y, x, core), rep: 4 (over z).
Axes of the slice: x: 2, y: 2, z: 4, core: 2. Of those that a mesh axis runs over, the one named last changes fastest.
Arguments:
- stale: bfloat16 [4096, 512], P(('blk', 'rep')), may hold values from -6 to 6
- w_self: bfloat16 [512, 512], replicated, may hold values from -0.25 to 0.25
- w_neigh: bfloat16 [512, 512], replicated, may hold values from -6 to 6
- tile_weights: bfloat16 [8, 4, 8, 3, 128, 128], P('blk', 'rep'), may hold values from 0 to 4, as said below
- tile_pos: int32 [8, 4, 8, 3], P('blk', 'rep'), may hold values from 0 to 3, as said below
- tile_counts: int32 [8, 4, 8], P('blk', 'rep'), may hold values from 0 to 3, as said below
Outputs:
- refreshed: bfloat16 [4096, 512], P(('blk', 'rep'))
The draws below stay inside these ranges and needn't reach their ends.
Inputs may be any that keep to these rules, and one draw needn't show every extreme that they name: `tile_weights`: non-negative edge weights. `tile_pos`: distinct within the live head of every list. `tile_counts`: every device has one full list.
All inputs are finite; a program needn't handle non-finite values.
Results may differ from the reference program's by a relative error of at most 0.013.
Values may be sent and summed in bfloat16 or wider, within the bound.
A program may use at most 64 MiB of HBM per device.

```python
import jax
import jax.numpy as jnp
from jax import lax

D = 512
TILE = 128
SB = 128
GROUPS = 8
MEMBERS = 4
CAP = 3
NODES = 4096
N_BLK = 8
N_REP = 4


def draw_tile_weights(key, part):
    first_key, second_key = jax.random.split(key)
    tile_shape = (GROUPS, MEMBERS, GROUPS, CAP, TILE, TILE)
    present = jax.random.uniform(first_key, tile_shape, jnp.float32) < 0.25
    strength = jnp.exp(jax.random.uniform(second_key, tile_shape, jnp.float32, jnp.log(0.25), jnp.log(4.0)))
    return jnp.where(present, strength, 0.0).astype(jnp.bfloat16)


def draw_tile_pos(key, part):
    pair_count = SB * MEMBERS // TILE * (SB // TILE)
    sub_keys = jax.random.split(key, GROUPS * MEMBERS * GROUPS)
    orders = jax.vmap(lambda sub_key: jax.random.permutation(sub_key, pair_count)[:CAP])(sub_keys)
    return orders.reshape(GROUPS, MEMBERS, GROUPS, CAP).astype(jnp.int32)


def draw_tile_counts(key, part):
    first_key, second_key = jax.random.split(key)
    counts = jax.random.randint(first_key, (GROUPS, MEMBERS, GROUPS), 0, CAP + 1, dtype=jnp.int32)
    full_shard = jax.random.randint(second_key, (GROUPS, MEMBERS, 1), 0, GROUPS, dtype=jnp.int32)
    return jnp.where(jnp.arange(GROUPS, dtype=jnp.int32)[None, None, :] == full_shard, CAP, counts).astype(jnp.int32)


def levels(stream_key, extent, pieces, least, largest):
    level, own = 1.0, jax.random.fold_in(stream_key, 6)
    for dim, blocks in pieces:
        heights = jnp.exp(jax.random.uniform(jax.random.fold_in(own, dim), (blocks,), jnp.float32, least / len(pieces), largest / len(pieces)))
        level = level * jnp.repeat(heights, extent[dim] // blocks).reshape([-1 if axis == dim else 1 for axis in range(len(extent))])
    return level


def scatter_about(own_key, shape, scale, most, cuts=(), held_as=jnp.bfloat16):
    values = jax.random.normal(own_key, shape, jnp.float32) * scale
    if len(cuts) > 0:
        values = levels(own_key, shape, cuts, -0.22, 0.18) * values
    return jnp.clip(values, min=-most, max=most).astype(held_as)


def setup_inputs(seed: int = 0) -> dict:
    key_list = jax.random.split(jax.random.key(seed), 7)
    stale = scatter_about(key_list[0], (NODES, D), 1.0, 6.0, ((0, 32),))
    w_self = scatter_about(key_list[1], (D, D), D ** -0.5, 0.25)
    w_neigh = scatter_about(key_list[2], (D, D), (max(1, D * 8 // (N_BLK * N_REP * TILE))) ** -0.5, 6.0)
    tile_weights = draw_tile_weights(jax.random.fold_in(key_list[6], 71), 0)
    tile_pos = draw_tile_pos(jax.random.fold_in(key_list[6], 71), 0)
    tile_counts = draw_tile_counts(jax.random.fold_in(key_list[6], 71), 0)
    return dict(stale=stale, w_self=w_self, w_neigh=w_neigh, tile_weights=tile_weights, tile_pos=tile_pos, tile_counts=tile_counts)


def member_partial(sources, weights, places, counts):
    col_tiles = SB // TILE
    row_tiles = SB * MEMBERS // TILE

    def shard_step(running, inputs):
        totals, degree = running
        source_block, shard_tiles, shard_places, live_count = inputs
        live_mask = (jnp.arange(CAP) < live_count).astype(jnp.float32)
        tiles = shard_tiles.astype(jnp.float32) * live_mask[:, None, None]
        column = shard_places % col_tiles
        row_tile = shard_places // col_tiles
        picked = jnp.take(source_block.reshape(col_tiles, TILE, D), column, axis=0).astype(jnp.float32)
        products = jnp.einsum('kij,kjd->kid', tiles, picked, precision=lax.Precision.HIGHEST)
        onehot = (row_tile[None, :] == jnp.arange(row_tiles)[:, None]).astype(jnp.float32)
        totals = totals + jnp.dot(onehot, products.reshape(CAP, TILE * D), precision=lax.Precision.HIGHEST).reshape(row_tiles * TILE, D)
        degree = degree + jnp.dot(onehot, lax.optimization_barrier(jnp.sum(tiles, axis=2)), precision=lax.Precision.HIGHEST).reshape(row_tiles * TILE)
        return ((totals, degree), None)
    start = (jnp.zeros((SB * MEMBERS, D), jnp.float32), jnp.zeros((SB * MEMBERS,), jnp.float32))
    result, _ = lax.scan(shard_step, start, (sources, weights, places, counts))
    return result

def rounded(values):
    return lax.optimization_barrier(values.astype(jnp.bfloat16)).astype(jnp.float32)

def reference(stale, w_self, w_neigh, tile_weights, tile_pos, tile_counts):
    stale_view = stale.reshape(GROUPS, MEMBERS, SB, D)

    def group_step(unused, group_id):

        def member_step(running, member):
            sources = stale_view[:, member]
            part_sum, part_deg = member_partial(sources, tile_weights[group_id, member], tile_pos[group_id, member], tile_counts[group_id, member])
            return ((running[0] + rounded(part_sum), running[1] + rounded(part_deg)), None)
        start = (jnp.zeros((SB * MEMBERS, D), jnp.float32), jnp.zeros((SB * MEMBERS,), jnp.float32))
        (totals, degree), _ = lax.scan(member_step, start, jnp.arange(MEMBERS))
        own_rows = stale_view[group_id].reshape(SB * MEMBERS, D)
        neighbour_mean = ((own_rows.astype(jnp.float32) + totals) / (1.0 + degree)[:, None]).astype(jnp.bfloat16)
        hidden = jnp.dot(own_rows, w_self, preferred_element_type=jnp.float32) + jnp.dot(neighbour_mean, w_neigh, preferred_element_type=jnp.float32)
        active_out = jnp.maximum(hidden, 0.0)
        refreshed = active_out * lax.rsqrt(lax.optimization_barrier(jnp.mean(active_out * active_out, axis=-1, keepdims=True)) + 1e-05)
        return (unused, refreshed.astype(jnp.bfloat16))
    _, outputs = lax.scan(group_step, jnp.zeros((), jnp.float32), jnp.arange(GROUPS))
    return outputs.reshape(GROUPS * MEMBERS * SB, D)
```

```python
import functools

import jax
import jax.numpy as jnp
from jax import lax
from jax.experimental import pallas as pl
from jax.experimental.pallas import tpu as pltpu
from jax.sharding import PartitionSpec as P

MESH = pl.DeviceIdType.MESH
CHUNKS = 4


def refresh_kernel(
    blocks, members, stale_ref, w_self_hbm, w_neigh_hbm, weights_hbm, places_ref, counts_ref,
    out_ref,
    w_self, w_neigh, weights, adjacency, gathered, partial, arrived, deg_send, deg_recv, total,
    load_sem, g_send, g_recv, f_send, f_recv, p_send, p_recv, d_send, d_recv,
):
    own, width = stale_ref.shape
    cap, tile = weights_hbm.shape[3], weights_hbm.shape[4]
    col_tiles = own // tile
    chips = blocks // 2
    chunk = width // CHUNKS
    my_blk = lax.axis_index("blk")
    my_rep = lax.axis_index("rep")
    chip, core = my_blk // 2, my_blk % 2

    def load(slot, source, target):
        return pltpu.make_async_copy(source, target, load_sem.at[slot])

    loads = [
        load(0, weights_hbm.at[0, 0], weights.at[pl.ds(0, blocks)]),
        load(1, w_self_hbm, w_self),
        load(2, w_neigh_hbm, w_neigh),
    ]
    for copy in loads:
        copy.start()

    pair = {"blk": chip * 2 + 1 - core}
    def chip_at(offset):
        return {"blk": ((chip + offset) % chips) * 2 + core}
    def member_at(offset):
        return {"rep": (my_rep + offset) % members}

    barrier = pltpu.get_barrier_semaphore()
    peers = [member_at(d) for d in range(1, members)]
    peers += [chip_at(o) for o in range(1, chips)] + [pair]
    for peer in peers:
        pl.semaphore_signal(barrier, inc=1, device_id=peer, device_id_type=MESH)

    def columns(h):
        return pl.ds(h * chunk, chunk)

    def to_chip(h, o):
        return pltpu.make_async_remote_copy(
            src_ref=stale_ref.at[:, columns(h)], dst_ref=gathered.at[h, 2 * o],
            send_sem=g_send.at[h, o], recv_sem=g_recv.at[h, o],
            device_id=chip_at(o), device_id_type=MESH)

    def to_pair(h, o):
        source = stale_ref.at[:, columns(h)] if o == 0 else gathered.at[h, 2 * o]
        return pltpu.make_async_remote_copy(
            src_ref=source, dst_ref=gathered.at[h, 2 * o + 1],
            send_sem=f_send.at[h, o], recv_sem=f_recv.at[h, o],
            device_id=pair, device_id_type=MESH)

    def to_member(h, d):
        return pltpu.make_async_remote_copy(
            src_ref=partial.at[h, d], dst_ref=arrived.at[h, d - 1],
            send_sem=p_send.at[h, d - 1], recv_sem=p_recv.at[h, d - 1],
            device_id=member_at(d), device_id_type=MESH)

    def degree_to(d):
        return pltpu.make_async_remote_copy(
            src_ref=deg_send.at[d], dst_ref=deg_recv.at[d - 1],
            send_sem=d_send.at[d - 1], recv_sem=d_recv.at[d - 1],
            device_id=member_at(d), device_id_type=MESH)

    pl.semaphore_wait(barrier, len(peers))
    for h in range(CHUNKS):
        for o in range(1, chips):
            to_chip(h, o).start()
        to_pair(h, 0).start()

    for h in range(CHUNKS):
        gathered[h, 0] = stale_ref[:, h * chunk:(h + 1) * chunk]
    weights[blocks] = jnp.zeros_like(weights[blocks])

    loads[0].wait()
    def place_tiles(slot):
        source = ((chip + chips - slot // 2) % chips) * 2 + (core + slot % 2) % 2
        live = counts_ref[0, 0, source]
        spots = [
            jnp.where(k < live, places_ref[0, k, 0, source], -1) for k in range(cap)
        ]
        for q in range(members * col_tiles):
            row = ((my_rep + q // col_tiles) % members) * col_tiles + q % col_tiles
            for column in range(col_tiles):
                spot = row * col_tiles + column
                block, index = jnp.int32(blocks), jnp.int32(0)
                for k in range(cap):
                    hit = spots[k] == spot
                    block = jnp.where(hit, source, block)
                    index = jnp.where(hit, k, index)
                start = slot * own + column * tile
                if not isinstance(slot, int):
                    start = pl.multiple_of(start, tile)
                adjacency[q * tile:(q + 1) * tile, pl.ds(start, tile)] = weights[block, index]

    if blocks <= 8:
        for slot in range(blocks):
            place_tiles(slot)
    else:
        @pl.loop(0, blocks)
        def _(slot):
            place_tiles(slot)

    ones = jnp.ones((16, blocks * own), jnp.bfloat16)
    for d in range(members):
        deg_send[d] = lax.dot_general(
            ones, adjacency[d * own:(d + 1) * own, :], (((1,), (1,)), ((), ())),
            preferred_element_type=jnp.float32).astype(jnp.bfloat16)
    for d in range(1, members):
        degree_to(d).start()

    group = min(members, max(1, 512 // own))
    for h in range(CHUNKS):
        for o in range(1, chips):
            to_chip(h, o).wait_recv()
            to_pair(h, o).start()
        for o in range(chips):
            to_pair(h, o).wait_recv()
        sources = gathered[h].reshape(blocks * own, chunk)
        for first in range(0, members, group):
            last = min(first + group, members)
            sums = jnp.dot(adjacency[first * own:last * own, :], sources,
                           preferred_element_type=jnp.float32).astype(jnp.bfloat16)
            partial[h, first:last] = sums.reshape(last - first, own, chunk)
            for d in range(max(first, 1), last):
                to_member(h, d).start()

    loads[1].wait()
    total[...] = jnp.dot(stale_ref[...], w_self[...], preferred_element_type=jnp.float32)
    degree = deg_send[0].astype(jnp.float32)
    for d in range(1, members):
        degree_to(d).wait_recv()
        degree = degree + deg_recv[d - 1].astype(jnp.float32)
    inverse = jnp.transpose(jnp.broadcast_to(1.0 / (1.0 + degree[0:1]), (own, own)))[:, 0:1]
    loads[2].wait()
    for h in range(CHUNKS):
        summed = partial[h, 0].astype(jnp.float32)
        for d in range(1, members):
            to_member(h, d).wait_recv()
            summed = summed + arrived[h, d - 1].astype(jnp.float32)
        own_rows = stale_ref[:, h * chunk:(h + 1) * chunk].astype(jnp.float32)
        mean = ((own_rows + summed) * inverse).astype(jnp.bfloat16)
        total[...] += jnp.dot(mean, w_neigh[h * chunk:(h + 1) * chunk, :],
                              preferred_element_type=jnp.float32)
    active = jnp.maximum(total[...], 0.0)
    scale = lax.rsqrt(jnp.mean(active * active, axis=-1, keepdims=True) + 1e-05)
    out_ref[...] = (active * scale).astype(out_ref.dtype)

    for h in range(CHUNKS):
        for o in range(1, chips):
            to_chip(h, o).wait_send()
        for o in range(chips):
            to_pair(h, o).wait_send()
        for d in range(1, members):
            to_member(h, d).wait_send()
    for d in range(1, members):
        degree_to(d).wait_send()


def on_device(stale, w_self, w_neigh, tile_weights, tile_pos, tile_counts):
    blocks = lax.axis_size("blk")
    members = lax.axis_size("rep")
    own, width = stale.shape
    cap, tile = tile_weights.shape[3], tile_weights.shape[4]
    chips = blocks // 2
    chunk = width // CHUNKS
    bf16, f32 = jnp.bfloat16, jnp.float32
    dma = pltpu.SemaphoreType.DMA
    vmem = pl.BlockSpec(memory_space=pltpu.VMEM)
    smem = pl.BlockSpec(memory_space=pltpu.SMEM)
    hbm = pl.BlockSpec(memory_space=pl.ANY)
    flops = 2 * own * width * (members * own * blocks + 2 * width)
    return pl.pallas_call(
        functools.partial(refresh_kernel, blocks, members),
        out_shape=jax.ShapeDtypeStruct((own, width), bf16),
        in_specs=[vmem, hbm, hbm, hbm, smem, smem],
        out_specs=vmem,
        scratch_shapes=[
            pltpu.VMEM(w_self.shape, bf16),
            pltpu.VMEM(w_neigh.shape, bf16),
            pltpu.VMEM((blocks + 1, cap, tile, tile), bf16),
            pltpu.VMEM((members * own, blocks * own), bf16),
            pltpu.VMEM((CHUNKS, blocks, own, chunk), bf16),
            pltpu.VMEM((CHUNKS, members, own, chunk), bf16),
            pltpu.VMEM((CHUNKS, members - 1, own, chunk), bf16),
            pltpu.VMEM((members, 16, own), bf16),
            pltpu.VMEM((members - 1, 16, own), bf16),
            pltpu.VMEM((own, width), f32),
            dma((3,)),
            dma((CHUNKS, chips)),
            dma((CHUNKS, chips)),
            dma((CHUNKS, chips)),
            dma((CHUNKS, chips)),
            dma((CHUNKS, members - 1)),
            dma((CHUNKS, members - 1)),
            dma((members - 1,)),
            dma((members - 1,)),
        ],
        compiler_params=pltpu.CompilerParams(
            collective_id=0, has_side_effects=True, vmem_limit_bytes=60 * 1024 * 1024),
        cost_estimate=pl.CostEstimate(
            flops=flops, bytes_accessed=2 * (tile_weights.size + 4 * own * width), transcendentals=own),
        name="refresh",
    )(stale, w_self, w_neigh, tile_weights, jnp.transpose(tile_pos, (0, 3, 1, 2)), tile_counts)


def solution(mesh):
    return jax.shard_map(
        on_device,
        mesh=mesh,
        in_specs=(
            P(("blk", "rep"), None),
            P(),
            P(),
            P("blk", "rep", None, None, None, None),
            P("blk", "rep", None, None),
            P("blk", "rep", None),
        ),
        out_specs=P(("blk", "rep"), None),
        check_vma=False,
    )
```

```python
import functools

import jax
import jax.numpy as jnp
from jax import lax
from jax.experimental import pallas as pl
from jax.experimental.pallas import tpu as pltpu
from jax.sharding import PartitionSpec as P

MESH = pl.DeviceIdType.MESH
CHUNKS = 4


def refresh_kernel(
    blocks, members, stale_hbm, w_self_hbm, w_neigh_hbm, weights_hbm, places_hbm, counts_hbm,
    out_ref,
    places_ref, counts_ref, w_self, w_neigh, weights, adjacency, gathered, partial, arrived, deg_send, deg_recv, total,
    load_sem, g_send, g_recv, f_send, f_recv, p_send, p_recv, d_send, d_recv,
):
    own, width = stale_hbm.shape
    cap, tile = weights_hbm.shape[3], weights_hbm.shape[4]
    col_tiles = own // tile
    chips = blocks // 2
    chunk = width // CHUNKS
    my_blk = lax.axis_index("blk")
    my_rep = lax.axis_index("rep")
    chip, core = my_blk // 2, my_blk % 2

    def load(slot, source, target):
        return pltpu.make_async_copy(source, target, load_sem.at[slot])

    own_loads = [
        load(h, stale_hbm.at[:, pl.ds(h * chunk, chunk)], gathered.at[h, 0])
        for h in range(CHUNKS)
    ]
    place_load = load(CHUNKS, places_hbm, places_ref)
    count_load = load(CHUNKS + 1, counts_hbm, counts_ref)
    tile_load = load(CHUNKS + 2, weights_hbm.at[0, 0], weights.at[pl.ds(0, blocks)])
    self_load = load(CHUNKS + 3, w_self_hbm, w_self)
    neigh_load = load(CHUNKS + 4, w_neigh_hbm, w_neigh)

    pair = {"blk": chip * 2 + 1 - core}
    def chip_at(offset):
        return {"blk": ((chip + offset) % chips) * 2 + core}
    def member_at(offset):
        return {"rep": (my_rep + offset) % members}

    barrier = pltpu.get_barrier_semaphore()
    peers = [member_at(d) for d in range(1, members)]
    peers += [chip_at(o) for o in range(1, chips)] + [pair]
    for peer in peers:
        pl.semaphore_signal(barrier, inc=1, device_id=peer, device_id_type=MESH)
    for copy in own_loads + [place_load, count_load, tile_load, self_load, neigh_load]:
        copy.start()

    def to_chip(h, o):
        return pltpu.make_async_remote_copy(
            src_ref=gathered.at[h, 0], dst_ref=gathered.at[h, 2 * o],
            send_sem=g_send.at[h, o], recv_sem=g_recv.at[h, o],
            device_id=chip_at(o), device_id_type=MESH)

    def to_pair(h, o):
        return pltpu.make_async_remote_copy(
            src_ref=gathered.at[h, 2 * o], dst_ref=gathered.at[h, 2 * o + 1],
            send_sem=f_send.at[h, o], recv_sem=f_recv.at[h, o],
            device_id=pair, device_id_type=MESH)

    def to_member(h, d):
        return pltpu.make_async_remote_copy(
            src_ref=partial.at[h, d], dst_ref=arrived.at[h, d - 1],
            send_sem=p_send.at[h, d - 1], recv_sem=p_recv.at[h, d - 1],
            device_id=member_at(d), device_id_type=MESH)

    def degree_to(d):
        return pltpu.make_async_remote_copy(
            src_ref=deg_send.at[d], dst_ref=deg_recv.at[d - 1],
            send_sem=d_send.at[d - 1], recv_sem=d_recv.at[d - 1],
            device_id=member_at(d), device_id_type=MESH)

    for copy in own_loads:
        copy.wait()
    pl.semaphore_wait(barrier, len(peers))
    for h in range(CHUNKS):
        for o in range(1, chips):
            to_chip(h, o).start()
        to_pair(h, 0).start()

    weights[blocks] = jnp.zeros_like(weights[blocks])

    place_load.wait()
    count_load.wait()
    tile_load.wait()
    def place_tiles(slot):
        source = ((chip + chips - slot // 2) % chips) * 2 + (core + slot % 2) % 2
        live = counts_ref[0, 0, source]
        spots = [
            jnp.where(k < live, places_ref[0, k, 0, source], -1) for k in range(cap)
        ]
        for q in range(members * col_tiles):
            row = ((my_rep + q // col_tiles) % members) * col_tiles + q % col_tiles
            for column in range(col_tiles):
                spot = row * col_tiles + column
                block, index = jnp.int32(blocks), jnp.int32(0)
                for k in range(cap):
                    hit = spots[k] == spot
                    block = jnp.where(hit, source, block)
                    index = jnp.where(hit, k, index)
                start = slot * own + column * tile
                if not isinstance(slot, int):
                    start = pl.multiple_of(start, tile)
                adjacency[q * tile:(q + 1) * tile, pl.ds(start, tile)] = weights[block, index]

    if blocks <= 8:
        for slot in range(blocks):
            place_tiles(slot)
    else:
        @pl.loop(0, blocks)
        def _(slot):
            place_tiles(slot)

    group = min(members, max(1, 512 // own))
    for h in range(CHUNKS):
        for o in range(1, chips):
            to_chip(h, o).wait_recv()
            to_pair(h, o).start()
        for o in range(chips):
            to_pair(h, o).wait_recv()
        sources = gathered[h].reshape(blocks * own, chunk)
        for first in range(0, members, group):
            last = min(first + group, members)
            sums = jnp.dot(adjacency[first * own:last * own, :], sources,
                           preferred_element_type=jnp.float32).astype(jnp.bfloat16)
            partial[h, first:last] = sums.reshape(last - first, own, chunk)
            for d in range(max(first, 1), last):
                to_member(h, d).start()
        if h == 0:
            ones = jnp.ones((16, blocks * own), jnp.bfloat16)
            for d in range(members):
                deg_send[d] = lax.dot_general(
                    ones, adjacency[d * own:(d + 1) * own, :], (((1,), (1,)), ((), ())),
                    preferred_element_type=jnp.float32).astype(jnp.bfloat16)
            for d in range(1, members):
                degree_to(d).start()

    self_load.wait()
    total[...] = jnp.dot(gathered[0, 0], w_self[0:chunk, :], preferred_element_type=jnp.float32)
    for h in range(1, CHUNKS):
        total[...] += jnp.dot(gathered[h, 0], w_self[h * chunk:(h + 1) * chunk, :],
                              preferred_element_type=jnp.float32)
    degree = deg_send[0].astype(jnp.float32)
    for d in range(1, members):
        degree_to(d).wait_recv()
        degree = degree + deg_recv[d - 1].astype(jnp.float32)
    inverse = jnp.transpose(jnp.broadcast_to(1.0 / (1.0 + degree[0:1]), (own, own)))[:, 0:1]
    neigh_load.wait()
    for h in range(CHUNKS):
        summed = partial[h, 0].astype(jnp.float32)
        for d in range(1, members):
            to_member(h, d).wait_recv()
            summed = summed + arrived[h, d - 1].astype(jnp.float32)
        own_rows = gathered[h, 0].astype(jnp.float32)
        mean = ((own_rows + summed) * inverse).astype(jnp.bfloat16)
        total[...] += jnp.dot(mean, w_neigh[h * chunk:(h + 1) * chunk, :],
                              preferred_element_type=jnp.float32)
    active = jnp.maximum(total[...], 0.0)
    scale = lax.rsqrt(jnp.mean(active * active, axis=-1, keepdims=True) + 1e-05)
    out_ref[...] = (active * scale).astype(out_ref.dtype)

    for h in range(CHUNKS):
        for o in range(1, chips):
            to_chip(h, o).wait_send()
        for o in range(chips):
            to_pair(h, o).wait_send()
        for d in range(1, members):
            to_member(h, d).wait_send()
    for d in range(1, members):
        degree_to(d).wait_send()


def on_device(stale, w_self, w_neigh, tile_weights, tile_pos, tile_counts):
    blocks = lax.axis_size("blk")
    members = lax.axis_size("rep")
    own, width = stale.shape
    cap, tile = tile_weights.shape[3], tile_weights.shape[4]
    chips = blocks // 2
    chunk = width // CHUNKS
    bf16, f32 = jnp.bfloat16, jnp.float32
    dma = pltpu.SemaphoreType.DMA
    vmem = pl.BlockSpec(memory_space=pltpu.VMEM)
    hbm = pl.BlockSpec(memory_space=pl.ANY)
    flops = 2 * own * width * (members * own * blocks + 2 * width)
    return pl.pallas_call(
        functools.partial(refresh_kernel, blocks, members),
        out_shape=jax.ShapeDtypeStruct((own, width), bf16),
        in_specs=[hbm] * 6,
        out_specs=vmem,
        scratch_shapes=[
            pltpu.SMEM((1, cap, 1, blocks), jnp.int32),
            pltpu.SMEM((1, 1, blocks), jnp.int32),
            pltpu.VMEM(w_self.shape, bf16),
            pltpu.VMEM(w_neigh.shape, bf16),
            pltpu.VMEM((blocks + 1, cap, tile, tile), bf16),
            pltpu.VMEM((members * own, blocks * own), bf16),
            pltpu.VMEM((CHUNKS, blocks, own, chunk), bf16),
            pltpu.VMEM((CHUNKS, members, own, chunk), bf16),
            pltpu.VMEM((CHUNKS, members - 1, own, chunk), bf16),
            pltpu.VMEM((members, 16, own), bf16),
            pltpu.VMEM((members - 1, 16, own), bf16),
            pltpu.VMEM((own, width), f32),
            dma((CHUNKS + 5,)),
            dma((CHUNKS, chips)),
            dma((CHUNKS, chips)),
            dma((CHUNKS, chips)),
            dma((CHUNKS, chips)),
            dma((CHUNKS, members - 1)),
            dma((CHUNKS, members - 1)),
            dma((members - 1,)),
            dma((members - 1,)),
        ],
        compiler_params=pltpu.CompilerParams(
            collective_id=0, has_side_effects=True, vmem_limit_bytes=60 * 1024 * 1024),
        cost_estimate=pl.CostEstimate(
            flops=flops, bytes_accessed=2 * (tile_weights.size + 4 * own * width), transcendentals=own),
        name="refresh",
    )(stale, w_self, w_neigh, tile_weights, jnp.transpose(tile_pos, (0, 3, 1, 2)), tile_counts)


def solution(mesh):
    return jax.shard_map(
        on_device,
        mesh=mesh,
        in_specs=(
            P(("blk", "rep"), None),
            P(),
            P(),
            P("blk", "rep", None, None, None, None),
            P("blk", "rep", None, None),
            P("blk", "rep", None),
        ),
        out_specs=P(("blk", "rep"), None),
        check_vma=False,
    )
```

```python
import functools

import jax
import jax.numpy as jnp
from jax import lax
from jax.experimental import pallas as pl
from jax.experimental.pallas import tpu as pltpu
from jax.sharding import PartitionSpec as P

MESH = pl.DeviceIdType.MESH
CHUNKS = 4


def refresh_kernel(
    blocks, members, stale_hbm, w_self_hbm, w_neigh_hbm, weights_hbm, places_hbm, counts_hbm,
    out_ref,
    places_ref, counts_ref, w_self, w_neigh, weights, adjacency, gathered, partial, arrived, deg_send, deg_recv, relayed, total,
    load_sem, g_send, g_recv, f_send, f_recv, p_send, p_recv, d_send, d_recv, r_recv,
):
    own, width = stale_hbm.shape
    cap, tile = weights_hbm.shape[3], weights_hbm.shape[4]
    col_tiles = own // tile
    chips = blocks // 2
    chunk = width // CHUNKS
    my_blk = lax.axis_index("blk")
    my_rep = lax.axis_index("rep")
    chip, core = my_blk // 2, my_blk % 2

    def load(slot, source, target):
        return pltpu.make_async_copy(source, target, load_sem.at[slot])

    own_loads = [
        load(h, stale_hbm.at[:, pl.ds(h * chunk, chunk)], gathered.at[h, 0])
        for h in range(CHUNKS)
    ]
    place_load = load(CHUNKS, places_hbm, places_ref)
    count_load = load(CHUNKS + 1, counts_hbm, counts_ref)
    tile_load = load(CHUNKS + 2, weights_hbm.at[0, 0], weights.at[pl.ds(0, blocks)])
    self_load = load(CHUNKS + 3, w_self_hbm, w_self)
    neigh_load = load(CHUNKS + 4, w_neigh_hbm, w_neigh)

    pair = {"blk": chip * 2 + 1 - core}
    def chip_at(offset):
        return {"blk": ((chip + offset) % chips) * 2 + core}
    def member_at(offset):
        return {"rep": (my_rep + offset) % members}

    barrier = pltpu.get_barrier_semaphore()
    peers = [member_at(d) for d in range(1, members)]
    peers += [chip_at(o) for o in range(1, chips)] + [pair]
    for peer in peers:
        pl.semaphore_signal(barrier, inc=1, device_id=peer, device_id_type=MESH)
    for copy in own_loads + [place_load, count_load, tile_load, self_load, neigh_load]:
        copy.start()

    def to_chip(h, o):
        return pltpu.make_async_remote_copy(
            src_ref=gathered.at[h, 0], dst_ref=gathered.at[h, 2 * o],
            send_sem=g_send.at[h, o], recv_sem=g_recv.at[h, o],
            device_id=chip_at(o), device_id_type=MESH)

    def to_pair(h, o):
        return pltpu.make_async_remote_copy(
            src_ref=gathered.at[h, 2 * o], dst_ref=gathered.at[h, 2 * o + 1],
            send_sem=f_send.at[h, o], recv_sem=f_recv.at[h, o],
            device_id=pair, device_id_type=MESH)

    def to_member(h, d):
        return pltpu.make_async_remote_copy(
            src_ref=partial.at[h, d], dst_ref=arrived.at[h, d - 1],
            send_sem=p_send.at[h, d - 1], recv_sem=p_recv.at[h, d - 1],
            device_id=member_at(d), device_id_type=MESH)

    relaying = members >= 3
    def to_relay(h, side):
        d, helper = (members - 1, 1) if side == 0 else (1, members - 2)
        return pltpu.make_async_remote_copy(
            src_ref=partial.at[h, d], dst_ref=relayed.at[side, h],
            send_sem=p_send.at[h, d - 1], recv_sem=r_recv.at[side, h],
            device_id={"rep": helper}, device_id_type=MESH)

    def ends_at(d):
        found = []
        if relaying and d == members - 1:
            found.append((0, my_rep == 0))
        if relaying and d == 1:
            found.append((1, my_rep == members - 1))
        return found

    def helps_at(d):
        found = []
        if relaying and d == members - 2:
            found.append((0, my_rep == 1))
        if relaying and d == 2:
            found.append((1, my_rep == members - 2))
        return found

    def send_sums(h, d):
        direct = None
        for side, here in ends_at(d):
            pl.when(here)(lambda side=side: to_relay(h, side).start())
        for side, here in ends_at(d) + helps_at(d):
            direct = jnp.logical_not(here) if direct is None else direct & jnp.logical_not(here)
        if direct is None:
            to_member(h, d).start()
        else:
            pl.when(direct)(lambda: to_member(h, d).start())

    def help_ends(h):
        for d in range(1, members):
            for side, here in helps_at(d):
                @pl.when(here)
                def _(d=d, side=side):
                    to_relay(h, side).wait_recv()
                    both = partial[h, d].astype(jnp.float32) + relayed[side, h].astype(jnp.float32)
                    partial[h, d] = both.astype(jnp.bfloat16)
                    to_member(h, d).start()

    def wait_sums(h, d):
        spared = None
        if relaying and d == members - 1:
            spared = my_rep == members - 1
        if relaying and d == 1:
            spared = my_rep == 0
        if spared is None:
            to_member(h, d).wait_recv()
        else:
            pl.when(jnp.logical_not(spared))(lambda: to_member(h, d).wait_recv())

    def degree_to(d):
        return pltpu.make_async_remote_copy(
            src_ref=deg_send.at[d], dst_ref=deg_recv.at[d - 1],
            send_sem=d_send.at[d - 1], recv_sem=d_recv.at[d - 1],
            device_id=member_at(d), device_id_type=MESH)

    for copy in own_loads:
        copy.wait()
    pl.semaphore_wait(barrier, len(peers))
    for o in range(1, chips):
        to_chip(0, o).start()
    to_pair(0, 0).start()

    if relaying:
        for end, d in ((members - 1, members - 1), (0, 1)):
            @pl.when(my_rep == end)
            def _(d=d):
                for h in range(CHUNKS):
                    arrived[h, d - 1] = jnp.zeros_like(arrived[h, d - 1])
    weights[blocks] = jnp.zeros_like(weights[blocks])

    place_load.wait()
    count_load.wait()
    tile_load.wait()
    def place_tiles(slot):
        source = ((chip + chips - slot // 2) % chips) * 2 + (core + slot % 2) % 2
        live = counts_ref[0, 0, source]
        spots = [
            jnp.where(k < live, places_ref[0, k, 0, source], -1) for k in range(cap)
        ]
        for q in range(members * col_tiles):
            row = ((my_rep + q // col_tiles) % members) * col_tiles + q % col_tiles
            for column in range(col_tiles):
                spot = row * col_tiles + column
                block, index = jnp.int32(blocks), jnp.int32(0)
                for k in range(cap):
                    hit = spots[k] == spot
                    block = jnp.where(hit, source, block)
                    index = jnp.where(hit, k, index)
                start = slot * own + column * tile
                if not isinstance(slot, int):
                    start = pl.multiple_of(start, tile)
                adjacency[q * tile:(q + 1) * tile, pl.ds(start, tile)] = weights[block, index]

    if blocks <= 8:
        for slot in range(blocks):
            place_tiles(slot)
    else:
        @pl.loop(0, blocks)
        def _(slot):
            place_tiles(slot)

    group = min(members, max(1, 512 // own))
    for h in range(CHUNKS):
        if h + 1 < CHUNKS:
            for o in range(1, chips):
                to_chip(h, o).wait_send()
            for o in range(1, chips):
                to_chip(h + 1, o).start()
            to_pair(h + 1, 0).start()
        for o in range(1, chips):
            to_chip(h, o).wait_recv()
            to_pair(h, o).start()
        for o in range(chips):
            to_pair(h, o).wait_recv()
        sources = gathered[h].reshape(blocks * own, chunk)
        for first in range(0, members, group):
            last = min(first + group, members)
            sums = jnp.dot(adjacency[first * own:last * own, :], sources,
                           preferred_element_type=jnp.float32).astype(jnp.bfloat16)
            partial[h, first:last] = sums.reshape(last - first, own, chunk)
            for d in range(max(first, 1), last):
                send_sums(h, d)
        if h > 0:
            help_ends(h - 1)
        if h == 0:
            ones = jnp.ones((16, blocks * own), jnp.bfloat16)
            for d in range(members):
                deg_send[d] = lax.dot_general(
                    ones, adjacency[d * own:(d + 1) * own, :], (((1,), (1,)), ((), ())),
                    preferred_element_type=jnp.float32).astype(jnp.bfloat16)
            for d in range(1, members):
                degree_to(d).start()

    help_ends(CHUNKS - 1)
    self_load.wait()
    total[...] = jnp.dot(gathered[0, 0], w_self[0:chunk, :], preferred_element_type=jnp.float32)
    for h in range(1, CHUNKS):
        total[...] += jnp.dot(gathered[h, 0], w_self[h * chunk:(h + 1) * chunk, :],
                              preferred_element_type=jnp.float32)
    degree = deg_send[0].astype(jnp.float32)
    for d in range(1, members):
        degree_to(d).wait_recv()
        degree = degree + deg_recv[d - 1].astype(jnp.float32)
    inverse = jnp.transpose(jnp.broadcast_to(1.0 / (1.0 + degree[0:1]), (own, own)))[:, 0:1]
    neigh_load.wait()
    for h in range(CHUNKS):
        summed = partial[h, 0].astype(jnp.float32)
        for d in range(1, members):
            wait_sums(h, d)
            summed = summed + arrived[h, d - 1].astype(jnp.float32)
        own_rows = gathered[h, 0].astype(jnp.float32)
        mean = ((own_rows + summed) * inverse).astype(jnp.bfloat16)
        total[...] += jnp.dot(mean, w_neigh[h * chunk:(h + 1) * chunk, :],
                              preferred_element_type=jnp.float32)
    active = jnp.maximum(total[...], 0.0)
    scale = lax.rsqrt(jnp.mean(active * active, axis=-1, keepdims=True) + 1e-05)
    out_ref[...] = (active * scale).astype(out_ref.dtype)

    for h in range(CHUNKS):
        if h == CHUNKS - 1:
            for o in range(1, chips):
                to_chip(h, o).wait_send()
        for o in range(chips):
            to_pair(h, o).wait_send()
        for d in range(1, members):
            to_member(h, d).wait_send()
    for d in range(1, members):
        degree_to(d).wait_send()


def on_device(stale, w_self, w_neigh, tile_weights, tile_pos, tile_counts):
    blocks = lax.axis_size("blk")
    members = lax.axis_size("rep")
    own, width = stale.shape
    cap, tile = tile_weights.shape[3], tile_weights.shape[4]
    chips = blocks // 2
    chunk = width // CHUNKS
    bf16, f32 = jnp.bfloat16, jnp.float32
    dma = pltpu.SemaphoreType.DMA
    vmem = pl.BlockSpec(memory_space=pltpu.VMEM)
    hbm = pl.BlockSpec(memory_space=pl.ANY)
    flops = 2 * own * width * (members * own * blocks + 2 * width)
    return pl.pallas_call(
        functools.partial(refresh_kernel, blocks, members),
        out_shape=jax.ShapeDtypeStruct((own, width), bf16),
        in_specs=[hbm] * 6,
        out_specs=vmem,
        scratch_shapes=[
            pltpu.SMEM((1, cap, 1, blocks), jnp.int32),
            pltpu.SMEM((1, 1, blocks), jnp.int32),
            pltpu.VMEM(w_self.shape, bf16),
            pltpu.VMEM(w_neigh.shape, bf16),
            pltpu.VMEM((blocks + 1, cap, tile, tile), bf16),
            pltpu.VMEM((members * own, blocks * own), bf16),
            pltpu.VMEM((CHUNKS, blocks, own, chunk), bf16),
            pltpu.VMEM((CHUNKS, members, own, chunk), bf16),
            pltpu.VMEM((CHUNKS, members - 1, own, chunk), bf16),
            pltpu.VMEM((members, 16, own), bf16),
            pltpu.VMEM((members - 1, 16, own), bf16),
            pltpu.VMEM((2, CHUNKS, own, chunk), bf16),
            pltpu.VMEM((own, width), f32),
            dma((CHUNKS + 5,)),
            dma((CHUNKS, chips)),
            dma((CHUNKS, chips)),
            dma((CHUNKS, chips)),
            dma((CHUNKS, chips)),
            dma((CHUNKS, members - 1)),
            dma((CHUNKS, members - 1)),
            dma((members - 1,)),
            dma((members - 1,)),
            dma((2, CHUNKS)),
        ],
        compiler_params=pltpu.CompilerParams(
            collective_id=0, has_side_effects=True, vmem_limit_bytes=60 * 1024 * 1024),
        cost_estimate=pl.CostEstimate(
            flops=flops, bytes_accessed=2 * (tile_weights.size + 4 * own * width), transcendentals=own),
        name="refresh",
    )(stale, w_self, w_neigh, tile_weights, jnp.transpose(tile_pos, (0, 3, 1, 2)), tile_counts)


def solution(mesh):
    return jax.shard_map(
        on_device,
        mesh=mesh,
        in_specs=(
            P(("blk", "rep"), None),
            P(),
            P(),
            P("blk", "rep", None, None, None, None),
            P("blk", "rep", None, None),
            P("blk", "rep", None),
        ),
        out_specs=P(("blk", "rep"), None),
        check_vma=False,
    )
```

```python
import functools

import jax
import jax.numpy as jnp
from jax import lax
from jax.experimental import pallas as pl
from jax.experimental.pallas import tpu as pltpu
from jax.sharding import PartitionSpec as P

MESH = pl.DeviceIdType.MESH
CHUNKS = 4


def refresh_kernel(
    blocks, members, stale_hbm, w_self_hbm, w_neigh_hbm, weights_hbm, places_hbm, counts_hbm,
    out_ref,
    places_ref, counts_ref, w_self, w_neigh, weights, adjacency, gathered, partial, arrived, deg_send, deg_recv, relayed, total,
    load_sem, g_send, g_recv, f_send, f_recv, p_send, p_recv, d_send, d_recv, r_recv,
):
    own, width = stale_hbm.shape
    cap, tile = weights_hbm.shape[3], weights_hbm.shape[4]
    col_tiles = own // tile
    chips = blocks // 2
    chunk = width // CHUNKS
    my_blk = lax.axis_index("blk")
    my_rep = lax.axis_index("rep")
    chip, core = my_blk // 2, my_blk % 2

    def load(slot, source, target):
        return pltpu.make_async_copy(source, target, load_sem.at[slot])

    own_loads = [
        load(h, stale_hbm.at[:, pl.ds(h * chunk, chunk)], gathered.at[h, 0])
        for h in range(CHUNKS)
    ]
    place_load = load(CHUNKS, places_hbm, places_ref)
    count_load = load(CHUNKS + 1, counts_hbm, counts_ref)
    tile_load = load(CHUNKS + 2, weights_hbm.at[0, 0], weights.at[pl.ds(0, blocks)])
    self_load = load(CHUNKS + 3, w_self_hbm, w_self)
    neigh_load = load(CHUNKS + 4, w_neigh_hbm, w_neigh)

    pair = {"blk": chip * 2 + 1 - core}
    def chip_at(offset):
        return {"blk": ((chip + offset) % chips) * 2 + core}
    def member_at(offset):
        return {"rep": (my_rep + offset) % members}

    barrier = pltpu.get_barrier_semaphore()
    peers = [member_at(d) for d in range(1, members)]
    peers += [chip_at(o) for o in range(1, chips)] + [pair]
    for peer in peers:
        pl.semaphore_signal(barrier, inc=1, device_id=peer, device_id_type=MESH)
    for copy in own_loads + [place_load, count_load, tile_load, self_load, neigh_load]:
        copy.start()

    def to_chip(h, o):
        return pltpu.make_async_remote_copy(
            src_ref=gathered.at[h, 0], dst_ref=gathered.at[h, 2 * o],
            send_sem=g_send.at[h, o], recv_sem=g_recv.at[h, o],
            device_id=chip_at(o), device_id_type=MESH)

    def to_pair(h, o):
        return pltpu.make_async_remote_copy(
            src_ref=gathered.at[h, 2 * o], dst_ref=gathered.at[h, 2 * o + 1],
            send_sem=f_send.at[h, o], recv_sem=f_recv.at[h, o],
            device_id=pair, device_id_type=MESH)

    def to_member(h, d):
        return pltpu.make_async_remote_copy(
            src_ref=partial.at[h, d], dst_ref=arrived.at[h, d - 1],
            send_sem=p_send.at[h, d - 1], recv_sem=p_recv.at[h, d - 1],
            device_id=member_at(d), device_id_type=MESH)

    relaying = members >= 3
    def to_relay(h, side):
        d, helper = (members - 1, 1) if side == 0 else (1, members - 2)
        return pltpu.make_async_remote_copy(
            src_ref=partial.at[h, d], dst_ref=relayed.at[side, h],
            send_sem=p_send.at[h, d - 1], recv_sem=r_recv.at[side, h],
            device_id={"rep": helper}, device_id_type=MESH)

    def ends_at(d):
        found = []
        if relaying and d == members - 1:
            found.append((0, my_rep == 0))
        if relaying and d == 1:
            found.append((1, my_rep == members - 1))
        return found

    def helps_at(d):
        found = []
        if relaying and d == members - 2:
            found.append((0, my_rep == 1))
        if relaying and d == 2:
            found.append((1, my_rep == members - 2))
        return found

    def relay_sums(h, d):
        for side, here in ends_at(d):
            pl.when(here)(lambda side=side: to_relay(h, side).start())

    def send_sums(h, d):
        direct = None
        for side, here in ends_at(d) + helps_at(d):
            direct = jnp.logical_not(here) if direct is None else direct & jnp.logical_not(here)
        if direct is None:
            to_member(h, d).start()
        else:
            pl.when(direct)(lambda: to_member(h, d).start())

    def help_ends(h):
        for d in range(1, members):
            for side, here in helps_at(d):
                @pl.when(here)
                def _(d=d, side=side):
                    to_relay(h, side).wait_recv()
                    both = partial[h, d].astype(jnp.float32) + relayed[side, h].astype(jnp.float32)
                    partial[h, d] = both.astype(jnp.bfloat16)
                    to_member(h, d).start()

    def wait_sums(h, d):
        spared = None
        if relaying and d == members - 1:
            spared = my_rep == members - 1
        if relaying and d == 1:
            spared = my_rep == 0
        if spared is None:
            to_member(h, d).wait_recv()
        else:
            pl.when(jnp.logical_not(spared))(lambda: to_member(h, d).wait_recv())

    def degree_to(d):
        return pltpu.make_async_remote_copy(
            src_ref=deg_send.at[d], dst_ref=deg_recv.at[d - 1],
            send_sem=d_send.at[d - 1], recv_sem=d_recv.at[d - 1],
            device_id=member_at(d), device_id_type=MESH)

    for copy in own_loads:
        copy.wait()
    pl.semaphore_wait(barrier, len(peers))
    for o in range(1, chips):
        to_chip(0, o).start()
    to_pair(0, 0).start()

    if relaying:
        for end, d in ((members - 1, members - 1), (0, 1)):
            @pl.when(my_rep == end)
            def _(d=d):
                for h in range(CHUNKS):
                    arrived[h, d - 1] = jnp.zeros_like(arrived[h, d - 1])
    weights[blocks] = jnp.zeros_like(weights[blocks])

    place_load.wait()
    count_load.wait()
    tile_load.wait()
    def place_tiles(slot):
        source = ((chip + chips - slot // 2) % chips) * 2 + (core + slot % 2) % 2
        live = counts_ref[0, 0, source]
        spots = [
            jnp.where(k < live, places_ref[0, k, 0, source], -1) for k in range(cap)
        ]
        for q in range(members * col_tiles):
            row = ((my_rep + q // col_tiles) % members) * col_tiles + q % col_tiles
            for column in range(col_tiles):
                spot = row * col_tiles + column
                block, index = jnp.int32(blocks), jnp.int32(0)
                for k in range(cap):
                    hit = spots[k] == spot
                    block = jnp.where(hit, source, block)
                    index = jnp.where(hit, k, index)
                start = slot * own + column * tile
                if not isinstance(slot, int):
                    start = pl.multiple_of(start, tile)
                adjacency[q * tile:(q + 1) * tile, pl.ds(start, tile)] = weights[block, index]

    if blocks <= 8:
        for slot in range(blocks):
            place_tiles(slot)
    else:
        @pl.loop(0, blocks)
        def _(slot):
            place_tiles(slot)

    ones = jnp.ones((blocks * own, own), jnp.bfloat16)
    for d in range(members):
        row_sums = jnp.dot(adjacency[d * own:(d + 1) * own, :], ones,
                           preferred_element_type=jnp.float32)
        deg_send[d] = jnp.transpose(row_sums)[0:16].astype(jnp.bfloat16)
    for d in range(1, members):
        degree_to(d).start()

    for o in range(1, chips):
        to_chip(0, o).wait_send()
    for h in range(1, CHUNKS):
        for o in range(1, chips):
            to_chip(h, o).start()
        to_pair(h, 0).start()

    def forward(h):
        for o in range(1, chips):
            to_chip(h, o).wait_recv()
            to_pair(h, o).start()

    forward(0)
    group = min(members, max(1, 512 // own))
    for h in range(CHUNKS):
        if 0 < h < CHUNKS - 1:
            forward(h + 1)
        for o in range(chips):
            to_pair(h, o).wait_recv()
        sources = gathered[h].reshape(blocks * own, chunk)
        for first in range(0, members, group):
            last = min(first + group, members)
            sums = jnp.dot(adjacency[first * own:last * own, :], sources,
                           preferred_element_type=jnp.float32).astype(jnp.bfloat16)
            partial[h, first:last] = sums.reshape(last - first, own, chunk)
            for d in range(max(first, 1), last):
                relay_sums(h, d)
            for d in range(max(first, 1), last):
                send_sums(h, d)
        if h > 0:
            help_ends(h - 1)
        elif CHUNKS > 1:
            forward(1)

    self_load.wait()
    total[...] = jnp.dot(gathered[0, 0], w_self[0:chunk, :], preferred_element_type=jnp.float32)
    for h in range(1, CHUNKS):
        total[...] += jnp.dot(gathered[h, 0], w_self[h * chunk:(h + 1) * chunk, :],
                              preferred_element_type=jnp.float32)
    help_ends(CHUNKS - 1)
    degree = deg_send[0].astype(jnp.float32)
    for d in range(1, members):
        degree_to(d).wait_recv()
        degree = degree + deg_recv[d - 1].astype(jnp.float32)
    inverse = jnp.transpose(jnp.broadcast_to(1.0 / (1.0 + degree[0:1]), (own, own)))[:, 0:1]
    neigh_load.wait()
    for h in range(CHUNKS):
        summed = partial[h, 0].astype(jnp.float32)
        for d in range(1, members):
            wait_sums(h, d)
            summed = summed + arrived[h, d - 1].astype(jnp.float32)
        own_rows = gathered[h, 0].astype(jnp.float32)
        mean = ((own_rows + summed) * inverse).astype(jnp.bfloat16)
        total[...] += jnp.dot(mean, w_neigh[h * chunk:(h + 1) * chunk, :],
                              preferred_element_type=jnp.float32)
    active = jnp.maximum(total[...], 0.0)
    scale = lax.rsqrt(jnp.mean(active * active, axis=-1, keepdims=True) + 1e-05)
    out_ref[...] = (active * scale).astype(out_ref.dtype)

    for h in range(CHUNKS):
        for o in range(1, chips):
            if h > 0:
                to_chip(h, o).wait_send()
        for o in range(chips):
            to_pair(h, o).wait_send()
        for d in range(1, members):
            to_member(h, d).wait_send()
    for d in range(1, members):
        degree_to(d).wait_send()


def on_device(stale, w_self, w_neigh, tile_weights, tile_pos, tile_counts):
    blocks = lax.axis_size("blk")
    members = lax.axis_size("rep")
    own, width = stale.shape
    cap, tile = tile_weights.shape[3], tile_weights.shape[4]
    chips = blocks // 2
    chunk = width // CHUNKS
    bf16, f32 = jnp.bfloat16, jnp.float32
    dma = pltpu.SemaphoreType.DMA
    vmem = pl.BlockSpec(memory_space=pltpu.VMEM)
    hbm = pl.BlockSpec(memory_space=pl.ANY)
    flops = 2 * own * width * (members * own * blocks + 2 * width)
    return pl.pallas_call(
        functools.partial(refresh_kernel, blocks, members),
        out_shape=jax.ShapeDtypeStruct((own, width), bf16),
        in_specs=[hbm] * 6,
        out_specs=vmem,
        scratch_shapes=[
            pltpu.SMEM((1, cap, 1, blocks), jnp.int32),
            pltpu.SMEM((1, 1, blocks), jnp.int32),
            pltpu.VMEM(w_self.shape, bf16),
            pltpu.VMEM(w_neigh.shape, bf16),
            pltpu.VMEM((blocks + 1, cap, tile, tile), bf16),
            pltpu.VMEM((members * own, blocks * own), bf16),
            pltpu.VMEM((CHUNKS, blocks, own, chunk), bf16),
            pltpu.VMEM((CHUNKS, members, own, chunk), bf16),
            pltpu.VMEM((CHUNKS, members - 1, own, chunk), bf16),
            pltpu.VMEM((members, 16, own), bf16),
            pltpu.VMEM((members - 1, 16, own), bf16),
            pltpu.VMEM((2, CHUNKS, own, chunk), bf16),
            pltpu.VMEM((own, width), f32),
            dma((CHUNKS + 5,)),
            dma((CHUNKS, chips)),
            dma((CHUNKS, chips)),
            dma((CHUNKS, chips)),
            dma((CHUNKS, chips)),
            dma((CHUNKS, members - 1)),
            dma((CHUNKS, members - 1)),
            dma((members - 1,)),
            dma((members - 1,)),
            dma((2, CHUNKS)),
        ],
        compiler_params=pltpu.CompilerParams(
            collective_id=0, has_side_effects=True, vmem_limit_bytes=60 * 1024 * 1024),
        cost_estimate=pl.CostEstimate(
            flops=flops, bytes_accessed=2 * (tile_weights.size + 4 * own * width), transcendentals=own),
        name="refresh",
    )(stale, w_self, w_neigh, tile_weights, jnp.transpose(tile_pos, (0, 3, 1, 2)), tile_counts)


def solution(mesh):
    return jax.shard_map(
        on_device,
        mesh=mesh,
        in_specs=(
            P(("blk", "rep"), None),
            P(),
            P(),
            P("blk", "rep", None, None, None, None),
            P("blk", "rep", None, None),
            P("blk", "rep", None),
        ),
        out_specs=P(("blk", "rep"), None),
        check_vma=False,
    )
```

```python
import functools

import jax
import jax.numpy as jnp
from jax import lax
from jax.experimental import pallas as pl
from jax.experimental.pallas import tpu as pltpu
from jax.sharding import PartitionSpec as P

MESH = pl.DeviceIdType.MESH
CHUNKS = 4


def refresh_kernel(
    blocks, members, stale_hbm, w_self_hbm, w_neigh_hbm, weights_hbm, places_hbm, counts_hbm,
    out_ref,
    places_ref, counts_ref, w_self, w_neigh, weights, adjacency, gathered, partial, arrived, deg_send, deg_recv, relayed, total,
    load_sem, g_send, g_recv, f_send, f_recv, p_send, p_recv, d_send, d_recv, r_recv,
):
    own, width = stale_hbm.shape
    cap, tile = weights_hbm.shape[3], weights_hbm.shape[4]
    col_tiles = own // tile
    chips = blocks // 2
    chunk = width // CHUNKS
    my_blk = lax.axis_index("blk")
    my_rep = lax.axis_index("rep")
    chip, core = my_blk // 2, my_blk % 2

    def load(slot, source, target):
        return pltpu.make_async_copy(source, target, load_sem.at[slot])

    own_loads = [
        load(h, stale_hbm.at[:, pl.ds(h * chunk, chunk)], gathered.at[h, 0])
        for h in range(CHUNKS)
    ]
    place_load = load(CHUNKS, places_hbm, places_ref)
    count_load = load(CHUNKS + 1, counts_hbm, counts_ref)
    tile_load = load(CHUNKS + 2, weights_hbm.at[0, 0], weights.at[pl.ds(0, blocks)])
    self_load = load(CHUNKS + 3, w_self_hbm, w_self)
    neigh_load = load(CHUNKS + 4, w_neigh_hbm, w_neigh)

    pair = {"blk": chip * 2 + 1 - core}
    def across(offset, sign):
        if chips & (chips - 1):
            return (chip + chips + sign * offset) % chips
        other, bit = 0, 1
        while bit < chips:
            other = other + (chip // bit % 2 + offset // bit % 2) % 2 * bit
            bit *= 2
        return other
    def chip_at(offset):
        return {"blk": across(offset, 1) * 2 + core}
    def member_at(offset):
        return {"rep": (my_rep + offset) % members}

    barrier = pltpu.get_barrier_semaphore()
    peers = [member_at(d) for d in range(1, members)]
    peers += [chip_at(o) for o in range(1, chips)] + [pair]
    for peer in peers:
        pl.semaphore_signal(barrier, inc=1, device_id=peer, device_id_type=MESH)
    for copy in own_loads + [place_load, count_load, tile_load, self_load, neigh_load]:
        copy.start()

    def to_chip(h, o):
        return pltpu.make_async_remote_copy(
            src_ref=stale_hbm.at[:, pl.ds(h * chunk, chunk)], dst_ref=gathered.at[h, 2 * o],
            send_sem=g_send.at[h, o], recv_sem=g_recv.at[h, o],
            device_id=chip_at(o), device_id_type=MESH)

    def to_pair(h, o):
        source = stale_hbm.at[:, pl.ds(h * chunk, chunk)] if o == 0 else gathered.at[h, 2 * o]
        return pltpu.make_async_remote_copy(
            src_ref=source, dst_ref=gathered.at[h, 2 * o + 1],
            send_sem=f_send.at[h, o], recv_sem=f_recv.at[h, o],
            device_id=pair, device_id_type=MESH)

    def to_member(h, d):
        return pltpu.make_async_remote_copy(
            src_ref=partial.at[h, d], dst_ref=arrived.at[h, d - 1],
            send_sem=p_send.at[h, d - 1], recv_sem=p_recv.at[h, d - 1],
            device_id=member_at(d), device_id_type=MESH)

    def relaying(h):
        return members >= 3 and h < CHUNKS - 1
    def to_relay(h, side):
        d, helper = (members - 1, 1) if side == 0 else (1, members - 2)
        return pltpu.make_async_remote_copy(
            src_ref=partial.at[h, d], dst_ref=relayed.at[side, h],
            send_sem=p_send.at[h, d - 1], recv_sem=r_recv.at[side, h],
            device_id={"rep": helper}, device_id_type=MESH)

    def ends_at(h, d):
        found = []
        if relaying(h) and d == members - 1:
            found.append((0, my_rep == 0))
        if relaying(h) and d == 1:
            found.append((1, my_rep == members - 1))
        return found

    def helps_at(h, d):
        found = []
        if relaying(h) and d == members - 2:
            found.append((0, my_rep == 1))
        if relaying(h) and d == 2:
            found.append((1, my_rep == members - 2))
        return found

    def relay_sums(h, d):
        for side, here in ends_at(h, d):
            pl.when(here)(lambda side=side: to_relay(h, side).start())

    def send_sums(h, d):
        direct = None
        for side, here in ends_at(h, d) + helps_at(h, d):
            direct = jnp.logical_not(here) if direct is None else direct & jnp.logical_not(here)
        if direct is None:
            to_member(h, d).start()
        else:
            pl.when(direct)(lambda: to_member(h, d).start())

    def help_ends(h):
        for d in range(1, members):
            for side, here in helps_at(h, d):
                @pl.when(here)
                def _(d=d, side=side):
                    to_relay(h, side).wait_recv()
                    both = partial[h, d].astype(jnp.float32) + relayed[side, h].astype(jnp.float32)
                    partial[h, d] = both.astype(jnp.bfloat16)
                    to_member(h, d).start()

    def wait_sums(h, d):
        spared = None
        if relaying(h) and d == members - 1:
            spared = my_rep == members - 1
        if relaying(h) and d == 1:
            spared = my_rep == 0
        if spared is None:
            to_member(h, d).wait_recv()
        else:
            pl.when(jnp.logical_not(spared))(lambda: to_member(h, d).wait_recv())

    def degree_to(d):
        return pltpu.make_async_remote_copy(
            src_ref=deg_send.at[d], dst_ref=deg_recv.at[d - 1],
            send_sem=d_send.at[d - 1], recv_sem=d_recv.at[d - 1],
            device_id=member_at(d), device_id_type=MESH)

    pl.semaphore_wait(barrier, len(peers))
    for o in reversed(range(1, chips)):
        to_chip(0, o).start()
    to_pair(0, 0).start()

    if members >= 3:
        for end, d in ((members - 1, members - 1), (0, 1)):
            @pl.when(my_rep == end)
            def _(d=d):
                for h in range(CHUNKS):
                    if relaying(h):
                        arrived[h, d - 1] = jnp.zeros_like(arrived[h, d - 1])
    weights[blocks] = jnp.zeros_like(weights[blocks])

    place_load.wait()
    count_load.wait()
    tile_load.wait()
    def place_tiles(slot):
        source = across(slot // 2, -1) * 2 + (core + slot % 2) % 2
        live = counts_ref[0, 0, source]
        spots = [
            jnp.where(k < live, places_ref[0, k, 0, source], -1) for k in range(cap)
        ]
        for q in range(members * col_tiles):
            row = ((my_rep + q // col_tiles) % members) * col_tiles + q % col_tiles
            for column in range(col_tiles):
                spot = row * col_tiles + column
                block, index = jnp.int32(blocks), jnp.int32(0)
                for k in range(cap):
                    hit = spots[k] == spot
                    block = jnp.where(hit, source, block)
                    index = jnp.where(hit, k, index)
                start = slot * own + column * tile
                if not isinstance(slot, int):
                    start = pl.multiple_of(start, tile)
                adjacency[q * tile:(q + 1) * tile, pl.ds(start, tile)] = weights[block, index]

    if blocks <= 8:
        for slot in range(blocks):
            place_tiles(slot)
    else:
        @pl.loop(0, blocks)
        def _(slot):
            place_tiles(slot)

    ones = jnp.ones((blocks * own, own), jnp.bfloat16)
    for d in range(members):
        row_sums = jnp.dot(adjacency[d * own:(d + 1) * own, :], ones,
                           preferred_element_type=jnp.float32)
        deg_send[d] = jnp.transpose(row_sums)[0:16].astype(jnp.bfloat16)
    for d in range(1, members):
        degree_to(d).start()

    for o in range(1, chips):
        to_chip(0, o).wait_send()
    for h in range(1, CHUNKS):
        for o in reversed(range(1, chips)):
            to_chip(h, o).start()
        to_pair(h, 0).start()

    def forward(h):
        for o in range(1, chips):
            to_chip(h, o).wait_recv()
            to_pair(h, o).start()

    for copy in own_loads:
        copy.wait()
    forward(0)
    group = min(members, max(1, 512 // own))
    for h in range(CHUNKS):
        if 0 < h < CHUNKS - 1:
            forward(h + 1)
        for o in range(chips):
            to_pair(h, o).wait_recv()
        sources = gathered[h].reshape(blocks * own, chunk)
        for first in range(0, members, group):
            last = min(first + group, members)
            sums = jnp.dot(adjacency[first * own:last * own, :], sources,
                           preferred_element_type=jnp.float32).astype(jnp.bfloat16)
            partial[h, first:last] = sums.reshape(last - first, own, chunk)
            for d in range(max(first, 1), last):
                relay_sums(h, d)
            for d in range(max(first, 1), last):
                send_sums(h, d)
        if h > 0:
            help_ends(h - 1)
        elif CHUNKS > 1:
            forward(1)

    self_load.wait()
    total[...] = jnp.dot(gathered[0, 0], w_self[0:chunk, :], preferred_element_type=jnp.float32)
    for h in range(1, CHUNKS):
        total[...] += jnp.dot(gathered[h, 0], w_self[h * chunk:(h + 1) * chunk, :],
                              preferred_element_type=jnp.float32)
    help_ends(CHUNKS - 1)
    degree = deg_send[0].astype(jnp.float32)
    for d in range(1, members):
        degree_to(d).wait_recv()
        degree = degree + deg_recv[d - 1].astype(jnp.float32)
    inverse = jnp.transpose(jnp.broadcast_to(1.0 / (1.0 + degree[0:1]), (own, own)))[:, 0:1]
    neigh_load.wait()
    for h in range(CHUNKS):
        summed = partial[h, 0].astype(jnp.float32)
        for d in range(1, members):
            wait_sums(h, d)
            summed = summed + arrived[h, d - 1].astype(jnp.float32)
        own_rows = gathered[h, 0].astype(jnp.float32)
        mean = ((own_rows + summed) * inverse).astype(jnp.bfloat16)
        total[...] += jnp.dot(mean, w_neigh[h * chunk:(h + 1) * chunk, :],
                              preferred_element_type=jnp.float32)
    active = jnp.maximum(total[...], 0.0)
    scale = lax.rsqrt(jnp.mean(active * active, axis=-1, keepdims=True) + 1e-05)
    out_ref[...] = (active * scale).astype(out_ref.dtype)

    for h in range(CHUNKS):
        for o in range(1, chips):
            if h > 0:
                to_chip(h, o).wait_send()
        for o in range(chips):
            to_pair(h, o).wait_send()
        for d in range(1, members):
            to_member(h, d).wait_send()
    for d in range(1, members):
        degree_to(d).wait_send()


def on_device(stale, w_self, w_neigh, tile_weights, tile_pos, tile_counts):
    blocks = lax.axis_size("blk")
    members = lax.axis_size("rep")
    own, width = stale.shape
    cap, tile = tile_weights.shape[3], tile_weights.shape[4]
    chips = blocks // 2
    chunk = width // CHUNKS
    bf16, f32 = jnp.bfloat16, jnp.float32
    dma = pltpu.SemaphoreType.DMA
    vmem = pl.BlockSpec(memory_space=pltpu.VMEM)
    hbm = pl.BlockSpec(memory_space=pl.ANY)
    flops = 2 * own * width * (members * own * blocks + 2 * width)
    return pl.pallas_call(
        functools.partial(refresh_kernel, blocks, members),
        out_shape=pltpu.VMEM((own, width), bf16),
        in_specs=[hbm] * 6,
        out_specs=vmem,
        scratch_shapes=[
            pltpu.SMEM((1, cap, 1, blocks), jnp.int32),
            pltpu.SMEM((1, 1, blocks), jnp.int32),
            pltpu.VMEM(w_self.shape, bf16),
            pltpu.VMEM(w_neigh.shape, bf16),
            pltpu.VMEM((blocks + 1, cap, tile, tile), bf16),
            pltpu.VMEM((members * own, blocks * own), bf16),
            pltpu.VMEM((CHUNKS, blocks, own, chunk), bf16),
            pltpu.VMEM((CHUNKS, members, own, chunk), bf16),
            pltpu.VMEM((CHUNKS, members - 1, own, chunk), bf16),
            pltpu.VMEM((members, 16, own), bf16),
            pltpu.VMEM((members - 1, 16, own), bf16),
            pltpu.VMEM((2, CHUNKS, own, chunk), bf16),
            pltpu.VMEM((own, width), f32),
            dma((CHUNKS + 5,)),
            dma((CHUNKS, chips)),
            dma((CHUNKS, chips)),
            dma((CHUNKS, chips)),
            dma((CHUNKS, chips)),
            dma((CHUNKS, members - 1)),
            dma((CHUNKS, members - 1)),
            dma((members - 1,)),
            dma((members - 1,)),
            dma((2, CHUNKS)),
        ],
        compiler_params=pltpu.CompilerParams(
            collective_id=0, has_side_effects=True, vmem_limit_bytes=60 * 1024 * 1024),
        cost_estimate=pl.CostEstimate(
            flops=flops, bytes_accessed=2 * (tile_weights.size + 4 * own * width), transcendentals=own),
        name="refresh",
    )(stale, w_self, w_neigh, tile_weights, jnp.transpose(tile_pos, (0, 3, 1, 2)), tile_counts)


def solution(mesh):
    return jax.shard_map(
        on_device,
        mesh=mesh,
        in_specs=(
            P(("blk", "rep"), None),
            P(),
            P(),
            P("blk", "rep", None, None, None, None),
            P("blk", "rep", None, None),
            P("blk", "rep", None),
        ),
        out_specs=P(("blk", "rep"), None),
        check_vma=False,
    )
```

```python
import functools

import jax
import jax.numpy as jnp
from jax import lax
from jax.experimental import pallas as pl
from jax.experimental.pallas import tpu as pltpu
from jax.sharding import PartitionSpec as P

MESH = pl.DeviceIdType.MESH
CHUNKS = 4


def refresh_kernel(
    blocks, members, stale_hbm, w_self_hbm, w_neigh_hbm, weights_hbm, places_hbm, counts_hbm,
    out_ref,
    places_ref, counts_ref, w_self, w_neigh, weights, adjacency, gathered, partial, arrived, deg_send, deg_recv, relayed, total,
    load_sem, g_send, g_recv, f_send, f_recv, p_send, p_recv, d_send, d_recv, r_recv,
):
    own, width = stale_hbm.shape
    cap, tile = weights_hbm.shape[3], weights_hbm.shape[4]
    col_tiles = own // tile
    chips = blocks // 2
    chunk = width // CHUNKS
    my_blk = lax.axis_index("blk")
    my_rep = lax.axis_index("rep")
    chip, core = my_blk // 2, my_blk % 2

    def load(slot, source, target):
        return pltpu.make_async_copy(source, target, load_sem.at[slot])

    own_loads = [
        load(h, stale_hbm.at[:, pl.ds(h * chunk, chunk)], gathered.at[h, 0])
        for h in range(CHUNKS)
    ]
    place_load = load(CHUNKS, places_hbm, places_ref)
    count_load = load(CHUNKS + 1, counts_hbm, counts_ref)
    tile_load = load(CHUNKS + 2, weights_hbm.at[0, 0], weights.at[pl.ds(0, blocks)])
    self_load = load(CHUNKS + 3, w_self_hbm, w_self)
    neigh_load = load(CHUNKS + 4, w_neigh_hbm, w_neigh)

    pair = {"blk": chip * 2 + 1 - core}
    def across(offset, sign):
        if chips & (chips - 1):
            return (chip + chips + sign * offset) % chips
        other, bit = 0, 1
        while bit < chips:
            other = other + (chip // bit % 2 + offset // bit % 2) % 2 * bit
            bit *= 2
        return other
    def chip_at(offset):
        return {"blk": across(offset, 1) * 2 + core}
    def member_at(offset):
        return {"rep": (my_rep + offset) % members}

    barrier = pltpu.get_barrier_semaphore()
    peers = [member_at(d) for d in range(1, members)]
    peers += [chip_at(o) for o in range(1, chips)] + [pair]
    for peer in peers:
        pl.semaphore_signal(barrier, inc=1, device_id=peer, device_id_type=MESH)
    for copy in [place_load, count_load, tile_load]:
        copy.start()

    def to_chip(h, o):
        return pltpu.make_async_remote_copy(
            src_ref=stale_hbm.at[:, pl.ds(h * chunk, chunk)], dst_ref=gathered.at[h, 2 * o],
            send_sem=g_send.at[h, o], recv_sem=g_recv.at[h, o],
            device_id=chip_at(o), device_id_type=MESH)

    def to_pair(h, o):
        source = stale_hbm.at[:, pl.ds(h * chunk, chunk)] if o == 0 else gathered.at[h, 2 * o]
        return pltpu.make_async_remote_copy(
            src_ref=source, dst_ref=gathered.at[h, 2 * o + 1],
            send_sem=f_send.at[h, o], recv_sem=f_recv.at[h, o],
            device_id=pair, device_id_type=MESH)

    def to_member(h, d):
        return pltpu.make_async_remote_copy(
            src_ref=partial.at[h, d], dst_ref=arrived.at[h, d - 1],
            send_sem=p_send.at[h, d - 1], recv_sem=p_recv.at[h, d - 1],
            device_id=member_at(d), device_id_type=MESH)

    def relaying(h):
        return members >= 3 and h < CHUNKS - 1
    def to_relay(h, side):
        d, helper = (members - 1, 1) if side == 0 else (1, members - 2)
        return pltpu.make_async_remote_copy(
            src_ref=partial.at[h, d], dst_ref=relayed.at[side, h],
            send_sem=p_send.at[h, d - 1], recv_sem=r_recv.at[side, h],
            device_id={"rep": helper}, device_id_type=MESH)

    def ends_at(h, d):
        found = []
        if relaying(h) and d == members - 1:
            found.append((0, my_rep == 0))
        if relaying(h) and d == 1:
            found.append((1, my_rep == members - 1))
        return found

    def helps_at(h, d):
        found = []
        if relaying(h) and d == members - 2:
            found.append((0, my_rep == 1))
        if relaying(h) and d == 2:
            found.append((1, my_rep == members - 2))
        return found

    def relay_sums(h, d):
        for side, here in ends_at(h, d):
            pl.when(here)(lambda side=side: to_relay(h, side).start())

    def send_sums(h, d):
        direct = None
        for side, here in ends_at(h, d) + helps_at(h, d):
            direct = jnp.logical_not(here) if direct is None else direct & jnp.logical_not(here)
        if direct is None:
            to_member(h, d).start()
        else:
            pl.when(direct)(lambda: to_member(h, d).start())

    def help_ends(h):
        for d in range(1, members):
            for side, here in helps_at(h, d):
                @pl.when(here)
                def _(d=d, side=side):
                    to_relay(h, side).wait_recv()
                    both = partial[h, d].astype(jnp.float32) + relayed[side, h].astype(jnp.float32)
                    partial[h, d] = both.astype(jnp.bfloat16)
                    to_member(h, d).start()

    def wait_sums(h, d):
        spared = None
        if relaying(h) and d == members - 1:
            spared = my_rep == members - 1
        if relaying(h) and d == 1:
            spared = my_rep == 0
        if spared is None:
            to_member(h, d).wait_recv()
        else:
            pl.when(jnp.logical_not(spared))(lambda: to_member(h, d).wait_recv())

    def degree_to(d):
        return pltpu.make_async_remote_copy(
            src_ref=deg_send.at[d], dst_ref=deg_recv.at[d - 1],
            send_sem=d_send.at[d - 1], recv_sem=d_recv.at[d - 1],
            device_id=member_at(d), device_id_type=MESH)

    pl.semaphore_wait(barrier, len(peers))
    for o in reversed(range(1, chips)):
        to_chip(0, o).start()
    to_pair(0, 0).start()
    for copy in own_loads + [self_load, neigh_load]:
        copy.start()

    if members >= 3:
        for end, d in ((members - 1, members - 1), (0, 1)):
            @pl.when(my_rep == end)
            def _(d=d):
                for h in range(CHUNKS):
                    if relaying(h):
                        arrived[h, d - 1] = jnp.zeros_like(arrived[h, d - 1])
    weights[blocks] = jnp.zeros_like(weights[blocks])

    place_load.wait()
    count_load.wait()
    tile_load.wait()
    def place_tiles(slot):
        source = across(slot // 2, -1) * 2 + (core + slot % 2) % 2
        live = counts_ref[0, 0, source]
        spots = [
            jnp.where(k < live, places_ref[0, k, 0, source], -1) for k in range(cap)
        ]
        for q in range(members * col_tiles):
            row = ((my_rep + q // col_tiles) % members) * col_tiles + q % col_tiles
            for column in range(col_tiles):
                spot = row * col_tiles + column
                block, index = jnp.int32(blocks), jnp.int32(0)
                for k in range(cap):
                    hit = spots[k] == spot
                    block = jnp.where(hit, source, block)
                    index = jnp.where(hit, k, index)
                start = slot * own + column * tile
                if not isinstance(slot, int):
                    start = pl.multiple_of(start, tile)
                adjacency[q * tile:(q + 1) * tile, pl.ds(start, tile)] = weights[block, index]

    if blocks <= 8:
        for slot in range(blocks):
            place_tiles(slot)
    else:
        @pl.loop(0, blocks)
        def _(slot):
            place_tiles(slot)

    ones = jnp.ones((blocks * own, own), jnp.bfloat16)
    for d in range(members):
        row_sums = jnp.dot(adjacency[d * own:(d + 1) * own, :], ones,
                           preferred_element_type=jnp.float32)
        deg_send[d] = jnp.transpose(row_sums)[0:16].astype(jnp.bfloat16)
    for d in range(1, members):
        degree_to(d).start()

    for o in range(1, chips):
        to_chip(0, o).wait_send()
    for h in range(1, CHUNKS):
        for o in reversed(range(1, chips)):
            to_chip(h, o).start()
        to_pair(h, 0).start()

    def forward(h):
        for o in range(1, chips):
            to_chip(h, o).wait_recv()
            to_pair(h, o).start()

    for copy in own_loads:
        copy.wait()
    forward(0)
    group = min(members, max(1, 512 // own))
    for h in range(CHUNKS):
        if 0 < h < CHUNKS - 1:
            forward(h + 1)
        for o in range(chips):
            to_pair(h, o).wait_recv()
        sources = gathered[h].reshape(blocks * own, chunk)
        for first in range(0, members, group):
            last = min(first + group, members)
            sums = jnp.dot(adjacency[first * own:last * own, :], sources,
                           preferred_element_type=jnp.float32).astype(jnp.bfloat16)
            partial[h, first:last] = sums.reshape(last - first, own, chunk)
            for d in range(max(first, 1), last):
                relay_sums(h, d)
            low = my_rep * 2 < members
            @pl.when(low)
            def _(h=h, first=first, last=last):
                for d in reversed(range(max(first, 1), last)):
                    send_sums(h, d)
            @pl.when(jnp.logical_not(low))
            def _(h=h, first=first, last=last):
                for d in range(max(first, 1), last):
                    send_sums(h, d)
        if h > 0:
            help_ends(h - 1)
        elif CHUNKS > 1:
            forward(1)

    self_load.wait()
    total[...] = jnp.dot(gathered[0, 0], w_self[0:chunk, :], preferred_element_type=jnp.float32)
    for h in range(1, CHUNKS):
        total[...] += jnp.dot(gathered[h, 0], w_self[h * chunk:(h + 1) * chunk, :],
                              preferred_element_type=jnp.float32)
    help_ends(CHUNKS - 1)
    degree = deg_send[0].astype(jnp.float32)
    for d in range(1, members):
        degree_to(d).wait_recv()
        degree = degree + deg_recv[d - 1].astype(jnp.float32)
    inverse = jnp.transpose(jnp.broadcast_to(1.0 / (1.0 + degree[0:1]), (own, own)))[:, 0:1]
    neigh_load.wait()
    for h in range(CHUNKS):
        summed = partial[h, 0].astype(jnp.float32)
        for d in range(1, members):
            wait_sums(h, d)
            summed = summed + arrived[h, d - 1].astype(jnp.float32)
        own_rows = gathered[h, 0].astype(jnp.float32)
        mean = ((own_rows + summed) * inverse).astype(jnp.bfloat16)
        total[...] += jnp.dot(mean, w_neigh[h * chunk:(h + 1) * chunk, :],
                              preferred_element_type=jnp.float32)
    active = jnp.maximum(total[...], 0.0)
    scale = lax.rsqrt(jnp.mean(active * active, axis=-1, keepdims=True) + 1e-05)
    out_ref[...] = (active * scale).astype(out_ref.dtype)

    for h in range(CHUNKS):
        for o in range(1, chips):
            if h > 0:
                to_chip(h, o).wait_send()
        for o in range(chips):
            to_pair(h, o).wait_send()
        for d in range(1, members):
            to_member(h, d).wait_send()
    for d in range(1, members):
        degree_to(d).wait_send()


def on_device(stale, w_self, w_neigh, tile_weights, tile_pos, tile_counts):
    blocks = lax.axis_size("blk")
    members = lax.axis_size("rep")
    own, width = stale.shape
    cap, tile = tile_weights.shape[3], tile_weights.shape[4]
    chips = blocks // 2
    chunk = width // CHUNKS
    bf16, f32 = jnp.bfloat16, jnp.float32
    dma = pltpu.SemaphoreType.DMA
    vmem = pl.BlockSpec(memory_space=pltpu.VMEM)
    hbm = pl.BlockSpec(memory_space=pl.ANY)
    flops = 2 * own * width * (members * own * blocks + 2 * width)
    return pl.pallas_call(
        functools.partial(refresh_kernel, blocks, members),
        out_shape=pltpu.VMEM((own, width), bf16),
        in_specs=[hbm] * 6,
        out_specs=vmem,
        scratch_shapes=[
            pltpu.SMEM((1, cap, 1, blocks), jnp.int32),
            pltpu.SMEM((1, 1, blocks), jnp.int32),
            pltpu.VMEM(w_self.shape, bf16),
            pltpu.VMEM(w_neigh.shape, bf16),
            pltpu.VMEM((blocks + 1, cap, tile, tile), bf16),
            pltpu.VMEM((members * own, blocks * own), bf16),
            pltpu.VMEM((CHUNKS, blocks, own, chunk), bf16),
            pltpu.VMEM((CHUNKS, members, own, chunk), bf16),
            pltpu.VMEM((CHUNKS, members - 1, own, chunk), bf16),
            pltpu.VMEM((members, 16, own), bf16),
            pltpu.VMEM((members - 1, 16, own), bf16),
            pltpu.VMEM((2, CHUNKS, own, chunk), bf16),
            pltpu.VMEM((own, width), f32),
            dma((CHUNKS + 5,)),
            dma((CHUNKS, chips)),
            dma((CHUNKS, chips)),
            dma((CHUNKS, chips)),
            dma((CHUNKS, chips)),
            dma((CHUNKS, members - 1)),
            dma((CHUNKS, members - 1)),
            dma((members - 1,)),
            dma((members - 1,)),
            dma((2, CHUNKS)),
        ],
        compiler_params=pltpu.CompilerParams(
            collective_id=0, has_side_effects=True, vmem_limit_bytes=60 * 1024 * 1024),
        cost_estimate=pl.CostEstimate(
            flops=flops, bytes_accessed=2 * (tile_weights.size + 4 * own * width), transcendentals=own),
        name="refresh",
    )(stale, w_self, w_neigh, tile_weights, jnp.transpose(tile_pos, (0, 3, 1, 2)), tile_counts)


def solution(mesh):
    return jax.shard_map(
        on_device,
        mesh=mesh,
        in_specs=(
            P(("blk", "rep"), None),
            P(),
            P(),
            P("blk", "rep", None, None, None, None),
            P("blk", "rep", None, None),
            P("blk", "rep", None),
        ),
        out_specs=P(("blk", "rep"), None),
        check_vma=False,
    )
```

```python
import functools

import jax
import jax.numpy as jnp
from jax import lax
from jax.experimental import pallas as pl
from jax.experimental.pallas import tpu as pltpu
from jax.sharding import PartitionSpec as P

MESH = pl.DeviceIdType.MESH
CHUNKS = 2


def refresh_kernel(
    blocks, members, stale_hbm, w_self_hbm, w_neigh_hbm, weights_hbm, places_hbm, counts_hbm,
    out_ref,
    places_ref, counts_ref, w_self, w_neigh, weights, adjacency, gathered, partial, arrived, deg_send, deg_recv, relayed, total,
    load_sem, g_send, g_recv, f_send, f_recv, p_send, p_recv, d_send, d_recv, r_recv,
):
    own, width = stale_hbm.shape
    cap, tile = weights_hbm.shape[3], weights_hbm.shape[4]
    col_tiles = own // tile
    chips = blocks // 2
    chunk = width // CHUNKS
    my_blk = lax.axis_index("blk")
    my_rep = lax.axis_index("rep")
    chip, core = my_blk // 2, my_blk % 2

    def load(slot, source, target):
        return pltpu.make_async_copy(source, target, load_sem.at[slot])

    own_loads = [
        load(h, stale_hbm.at[:, pl.ds(h * chunk, chunk)], gathered.at[h, 0])
        for h in range(CHUNKS)
    ]
    place_load = load(CHUNKS, places_hbm, places_ref)
    count_load = load(CHUNKS + 1, counts_hbm, counts_ref)
    tile_load = load(CHUNKS + 2, weights_hbm.at[0, 0], weights.at[pl.ds(0, blocks)])
    self_load = load(CHUNKS + 3, w_self_hbm, w_self)
    neigh_load = load(CHUNKS + 4, w_neigh_hbm, w_neigh)

    pair = {"blk": chip * 2 + 1 - core}
    def across(offset, sign):
        if chips & (chips - 1):
            return (chip + chips + sign * offset) % chips
        other, bit = 0, 1
        while bit < chips:
            other = other + (chip // bit % 2 + offset // bit % 2) % 2 * bit
            bit *= 2
        return other
    def chip_at(offset):
        return {"blk": across(offset, 1) * 2 + core}
    def member_at(offset):
        return {"rep": (my_rep + offset) % members}

    barrier = pltpu.get_barrier_semaphore()
    peers = [member_at(d) for d in range(1, members)]
    peers += [chip_at(o) for o in range(1, chips)] + [pair]
    for peer in peers:
        pl.semaphore_signal(barrier, inc=1, device_id=peer, device_id_type=MESH)
    for copy in [place_load, count_load, tile_load]:
        copy.start()

    def to_chip(h, o):
        return pltpu.make_async_remote_copy(
            src_ref=stale_hbm.at[:, pl.ds(h * chunk, chunk)], dst_ref=gathered.at[h, 2 * o],
            send_sem=g_send.at[h, o], recv_sem=g_recv.at[h, o],
            device_id=chip_at(o), device_id_type=MESH)

    def to_pair(h, o):
        source = stale_hbm.at[:, pl.ds(h * chunk, chunk)] if o == 0 else gathered.at[h, 2 * o]
        return pltpu.make_async_remote_copy(
            src_ref=source, dst_ref=gathered.at[h, 2 * o + 1],
            send_sem=f_send.at[h, o], recv_sem=f_recv.at[h, o],
            device_id=pair, device_id_type=MESH)

    def to_member(h, d):
        return pltpu.make_async_remote_copy(
            src_ref=partial.at[h, d], dst_ref=arrived.at[h, d - 1],
            send_sem=p_send.at[h, d - 1], recv_sem=p_recv.at[h, d - 1],
            device_id=member_at(d), device_id_type=MESH)

    def relaying(h):
        return members >= 3 and h < CHUNKS - 1
    def to_relay(h, side):
        d, helper = (members - 1, 1) if side == 0 else (1, members - 2)
        return pltpu.make_async_remote_copy(
            src_ref=partial.at[h, d], dst_ref=relayed.at[side, h],
            send_sem=p_send.at[h, d - 1], recv_sem=r_recv.at[side, h],
            device_id={"rep": helper}, device_id_type=MESH)

    def ends_at(h, d):
        found = []
        if relaying(h) and d == members - 1:
            found.append((0, my_rep == 0))
        if relaying(h) and d == 1:
            found.append((1, my_rep == members - 1))
        return found

    def helps_at(h, d):
        found = []
        if relaying(h) and d == members - 2:
            found.append((0, my_rep == 1))
        if relaying(h) and d == 2:
            found.append((1, my_rep == members - 2))
        return found

    def relay_sums(h, d):
        for side, here in ends_at(h, d):
            pl.when(here)(lambda side=side: to_relay(h, side).start())

    def send_sums(h, d):
        direct = None
        for side, here in ends_at(h, d) + helps_at(h, d):
            direct = jnp.logical_not(here) if direct is None else direct & jnp.logical_not(here)
        if direct is None:
            to_member(h, d).start()
        else:
            pl.when(direct)(lambda: to_member(h, d).start())

    def help_ends(h):
        for d in range(1, members):
            for side, here in helps_at(h, d):
                @pl.when(here)
                def _(d=d, side=side):
                    to_relay(h, side).wait_recv()
                    both = partial[h, d].astype(jnp.float32) + relayed[side, h].astype(jnp.float32)
                    partial[h, d] = both.astype(jnp.bfloat16)
                    to_member(h, d).start()

    def wait_sums(h, d):
        spared = None
        if relaying(h) and d == members - 1:
            spared = my_rep == members - 1
        if relaying(h) and d == 1:
            spared = my_rep == 0
        if spared is None:
            to_member(h, d).wait_recv()
        else:
            pl.when(jnp.logical_not(spared))(lambda: to_member(h, d).wait_recv())

    def degree_to(d):
        return pltpu.make_async_remote_copy(
            src_ref=deg_send.at[d], dst_ref=deg_recv.at[d - 1],
            send_sem=d_send.at[d - 1], recv_sem=d_recv.at[d - 1],
            device_id=member_at(d), device_id_type=MESH)

    pl.semaphore_wait(barrier, len(peers))
    for o in reversed(range(1, chips)):
        to_chip(0, o).start()
    to_pair(0, 0).start()
    for copy in own_loads + [self_load, neigh_load]:
        copy.start()

    if members >= 3:
        for end, d in ((members - 1, members - 1), (0, 1)):
            @pl.when(my_rep == end)
            def _(d=d):
                for h in range(CHUNKS):
                    if relaying(h):
                        arrived[h, d - 1] = jnp.zeros_like(arrived[h, d - 1])
    weights[blocks] = jnp.zeros_like(weights[blocks])

    place_load.wait()
    count_load.wait()
    tile_load.wait()
    def place_tiles(slot):
        source = across(slot // 2, -1) * 2 + (core + slot % 2) % 2
        live = counts_ref[0, 0, source]
        spots = [
            jnp.where(k < live, places_ref[0, k, 0, source], -1) for k in range(cap)
        ]
        for q in range(members * col_tiles):
            row = ((my_rep + q // col_tiles) % members) * col_tiles + q % col_tiles
            for column in range(col_tiles):
                spot = row * col_tiles + column
                block, index = jnp.int32(blocks), jnp.int32(0)
                for k in range(cap):
                    hit = spots[k] == spot
                    block = jnp.where(hit, source, block)
                    index = jnp.where(hit, k, index)
                start = slot * own + column * tile
                if not isinstance(slot, int):
                    start = pl.multiple_of(start, tile)
                adjacency[q * tile:(q + 1) * tile, pl.ds(start, tile)] = weights[block, index]

    if blocks <= 8:
        for slot in range(blocks):
            place_tiles(slot)
    else:
        @pl.loop(0, blocks)
        def _(slot):
            place_tiles(slot)

    ones = jnp.ones((blocks * own, own), jnp.bfloat16)
    for d in range(members):
        row_sums = jnp.dot(adjacency[d * own:(d + 1) * own, :], ones,
                           preferred_element_type=jnp.float32)
        deg_send[d] = jnp.transpose(row_sums)[0:16].astype(jnp.bfloat16)
    for d in range(1, members):
        degree_to(d).start()

    for o in range(1, chips):
        to_chip(0, o).wait_send()
    for h in range(1, CHUNKS):
        for o in reversed(range(1, chips)):
            to_chip(h, o).start()
        to_pair(h, 0).start()

    def forward(h):
        for o in range(1, chips):
            to_chip(h, o).wait_recv()
            to_pair(h, o).start()

    for copy in own_loads:
        copy.wait()
    forward(0)
    group = min(members, max(1, 512 // own))
    for h in range(CHUNKS):
        if 0 < h < CHUNKS - 1:
            forward(h + 1)
        for o in range(chips):
            to_pair(h, o).wait_recv()
        sources = gathered[h].reshape(blocks * own, chunk)
        for first in range(0, members, group):
            last = min(first + group, members)
            sums = jnp.dot(adjacency[first * own:last * own, :], sources,
                           preferred_element_type=jnp.float32).astype(jnp.bfloat16)
            partial[h, first:last] = sums.reshape(last - first, own, chunk)
            for d in range(max(first, 1), last):
                relay_sums(h, d)
            low = my_rep * 2 < members
            @pl.when(low)
            def _(h=h, first=first, last=last):
                for d in reversed(range(max(first, 1), last)):
                    send_sums(h, d)
            @pl.when(jnp.logical_not(low))
            def _(h=h, first=first, last=last):
                for d in range(max(first, 1), last):
                    send_sums(h, d)
        if h > 0:
            help_ends(h - 1)
        elif CHUNKS > 1:
            forward(1)

    self_load.wait()
    total[...] = jnp.dot(gathered[0, 0], w_self[0:chunk, :], preferred_element_type=jnp.float32)
    for h in range(1, CHUNKS):
        total[...] += jnp.dot(gathered[h, 0], w_self[h * chunk:(h + 1) * chunk, :],
                              preferred_element_type=jnp.float32)
    help_ends(CHUNKS - 1)
    degree = deg_send[0].astype(jnp.float32)
    for d in range(1, members):
        degree_to(d).wait_recv()
        degree = degree + deg_recv[d - 1].astype(jnp.float32)
    inverse = jnp.transpose(jnp.broadcast_to(1.0 / (1.0 + degree[0:1]), (own, own)))[:, 0:1]
    neigh_load.wait()
    for h in range(CHUNKS):
        summed = partial[h, 0].astype(jnp.float32)
        for d in range(1, members):
            wait_sums(h, d)
            summed = summed + arrived[h, d - 1].astype(jnp.float32)
        own_rows = gathered[h, 0].astype(jnp.float32)
        mean = ((own_rows + summed) * inverse).astype(jnp.bfloat16)
        total[...] += jnp.dot(mean, w_neigh[h * chunk:(h + 1) * chunk, :],
                              preferred_element_type=jnp.float32)
    active = jnp.maximum(total[...], 0.0)
    scale = lax.rsqrt(jnp.mean(active * active, axis=-1, keepdims=True) + 1e-05)
    out_ref[...] = (active * scale).astype(out_ref.dtype)

    for h in range(CHUNKS):
        for o in range(1, chips):
            if h > 0:
                to_chip(h, o).wait_send()
        for o in range(chips):
            to_pair(h, o).wait_send()
        for d in range(1, members):
            to_member(h, d).wait_send()
    for d in range(1, members):
        degree_to(d).wait_send()


def on_device(stale, w_self, w_neigh, tile_weights, tile_pos, tile_counts):
    blocks = lax.axis_size("blk")
    members = lax.axis_size("rep")
    own, width = stale.shape
    cap, tile = tile_weights.shape[3], tile_weights.shape[4]
    chips = blocks // 2
    chunk = width // CHUNKS
    bf16, f32 = jnp.bfloat16, jnp.float32
    dma = pltpu.SemaphoreType.DMA
    vmem = pl.BlockSpec(memory_space=pltpu.VMEM)
    hbm = pl.BlockSpec(memory_space=pl.ANY)
    flops = 2 * own * width * (members * own * blocks + 2 * width)
    return pl.pallas_call(
        functools.partial(refresh_kernel, blocks, members),
        out_shape=pltpu.VMEM((own, width), bf16),
        in_specs=[hbm] * 6,
        out_specs=vmem,
        scratch_shapes=[
            pltpu.SMEM((1, cap, 1, blocks), jnp.int32),
            pltpu.SMEM((1, 1, blocks), jnp.int32),
            pltpu.VMEM(w_self.shape, bf16),
            pltpu.VMEM(w_neigh.shape, bf16),
            pltpu.VMEM((blocks + 1, cap, tile, tile), bf16),
            pltpu.VMEM((members * own, blocks * own), bf16),
            pltpu.VMEM((CHUNKS, blocks, own, chunk), bf16),
            pltpu.VMEM((CHUNKS, members, own, chunk), bf16),
            pltpu.VMEM((CHUNKS, members - 1, own, chunk), bf16),
            pltpu.VMEM((members, 16, own), bf16),
            pltpu.VMEM((members - 1, 16, own), bf16),
            pltpu.VMEM((2, CHUNKS, own, chunk), bf16),
            pltpu.VMEM((own, width), f32),
            dma((CHUNKS + 5,)),
            dma((CHUNKS, chips)),
            dma((CHUNKS, chips)),
            dma((CHUNKS, chips)),
            dma((CHUNKS, chips)),
            dma((CHUNKS, members - 1)),
            dma((CHUNKS, members - 1)),
            dma((members - 1,)),
            dma((members - 1,)),
            dma((2, CHUNKS)),
        ],
        compiler_params=pltpu.CompilerParams(
            collective_id=0, has_side_effects=True, vmem_limit_bytes=60 * 1024 * 1024),
        cost_estimate=pl.CostEstimate(
            flops=flops, bytes_accessed=2 * (tile_weights.size + 4 * own * width), transcendentals=own),
        name="refresh",
    )(stale, w_self, w_neigh, tile_weights, jnp.transpose(tile_pos, (0, 3, 1, 2)), tile_counts)


def solution(mesh):
    return jax.shard_map(
        on_device,
        mesh=mesh,
        in_specs=(
            P(("blk", "rep"), None),
            P(),
            P(),
            P("blk", "rep", None, None, None, None),
            P("blk", "rep", None, None),
            P("blk", "rep", None),
        ),
        out_specs=P(("blk", "rep"), None),
        check_vma=False,
    )
```

```python
import functools

import jax
import jax.numpy as jnp
from jax import lax
from jax.experimental import pallas as pl
from jax.experimental.pallas import tpu as pltpu
from jax.sharding import PartitionSpec as P

MESH = pl.DeviceIdType.MESH
QUARTERS = (1, 2, 1)
CHUNKS = len(QUARTERS)


def chunk_of(width, h):
    unit = width // sum(QUARTERS)
    return sum(QUARTERS[:h]) * unit, QUARTERS[h] * unit


def refresh_kernel(
    blocks, members, stale_hbm, w_self_hbm, w_neigh_hbm, weights_hbm, places_hbm, counts_hbm,
    out_ref,
    places_ref, counts_ref, w_self, w_neigh, weights, adjacency, gathered, partial, arrived, deg_send, deg_recv, relayed, total,
    load_sem, g_send, g_recv, f_send, f_recv, p_send, p_recv, d_send, d_recv, r_recv,
):
    own, width = stale_hbm.shape
    cap, tile = weights_hbm.shape[3], weights_hbm.shape[4]
    col_tiles = own // tile
    chips = blocks // 2
    my_blk = lax.axis_index("blk")
    my_rep = lax.axis_index("rep")
    chip, core = my_blk // 2, my_blk % 2

    def columns(h):
        return pl.ds(*chunk_of(width, h))

    def load(slot, source, target):
        return pltpu.make_async_copy(source, target, load_sem.at[slot])

    own_loads = [
        load(h, stale_hbm.at[:, columns(h)], gathered[h].at[0])
        for h in range(CHUNKS)
    ]
    place_load = load(CHUNKS, places_hbm, places_ref)
    count_load = load(CHUNKS + 1, counts_hbm, counts_ref)
    tile_load = load(CHUNKS + 2, weights_hbm.at[0, 0], weights.at[pl.ds(0, blocks)])
    self_load = load(CHUNKS + 3, w_self_hbm, w_self)
    neigh_load = load(CHUNKS + 4, w_neigh_hbm, w_neigh)

    pair = {"blk": chip * 2 + 1 - core}
    def across(offset, sign):
        if chips & (chips - 1):
            return (chip + chips + sign * offset) % chips
        other, bit = 0, 1
        while bit < chips:
            other = other + (chip // bit % 2 + offset // bit % 2) % 2 * bit
            bit *= 2
        return other
    def chip_at(offset):
        return {"blk": across(offset, 1) * 2 + core}
    def member_at(offset):
        return {"rep": (my_rep + offset) % members}

    barrier = pltpu.get_barrier_semaphore()
    peers = [member_at(d) for d in range(1, members)]
    peers += [chip_at(o) for o in range(1, chips)] + [pair]
    for peer in peers:
        pl.semaphore_signal(barrier, inc=1, device_id=peer, device_id_type=MESH)
    for copy in [place_load, count_load, tile_load]:
        copy.start()

    def to_chip(h, o):
        return pltpu.make_async_remote_copy(
            src_ref=stale_hbm.at[:, columns(h)], dst_ref=gathered[h].at[2 * o],
            send_sem=g_send.at[h, o], recv_sem=g_recv.at[h, o],
            device_id=chip_at(o), device_id_type=MESH)

    def to_pair(h, o):
        source = stale_hbm.at[:, columns(h)] if o == 0 else gathered[h].at[2 * o]
        return pltpu.make_async_remote_copy(
            src_ref=source, dst_ref=gathered[h].at[2 * o + 1],
            send_sem=f_send.at[h, o], recv_sem=f_recv.at[h, o],
            device_id=pair, device_id_type=MESH)

    def to_member(h, d):
        return pltpu.make_async_remote_copy(
            src_ref=partial[h].at[d], dst_ref=arrived[h].at[d - 1],
            send_sem=p_send.at[h, d - 1], recv_sem=p_recv.at[h, d - 1],
            device_id=member_at(d), device_id_type=MESH)

    def relaying(h):
        return members >= 3 and h < CHUNKS - 1
    def to_relay(h, side):
        d, helper = (members - 1, 1) if side == 0 else (1, members - 2)
        return pltpu.make_async_remote_copy(
            src_ref=partial[h].at[d], dst_ref=relayed[h].at[side],
            send_sem=p_send.at[h, d - 1], recv_sem=r_recv.at[side, h],
            device_id={"rep": helper}, device_id_type=MESH)

    def ends_at(h, d):
        found = []
        if relaying(h) and d == members - 1:
            found.append((0, my_rep == 0))
        if relaying(h) and d == 1:
            found.append((1, my_rep == members - 1))
        return found

    def helps_at(h, d):
        found = []
        if relaying(h) and d == members - 2:
            found.append((0, my_rep == 1))
        if relaying(h) and d == 2:
            found.append((1, my_rep == members - 2))
        return found

    def relay_sums(h, d):
        for side, here in ends_at(h, d):
            pl.when(here)(lambda side=side: to_relay(h, side).start())

    def send_sums(h, d):
        direct = None
        for side, here in ends_at(h, d) + helps_at(h, d):
            direct = jnp.logical_not(here) if direct is None else direct & jnp.logical_not(here)
        if direct is None:
            to_member(h, d).start()
        else:
            pl.when(direct)(lambda: to_member(h, d).start())

    def help_ends(h):
        for d in range(1, members):
            for side, here in helps_at(h, d):
                @pl.when(here)
                def _(d=d, side=side):
                    to_relay(h, side).wait_recv()
                    both = partial[h][d].astype(jnp.float32) + relayed[h][side].astype(jnp.float32)
                    partial[h][d] = both.astype(jnp.bfloat16)
                    to_member(h, d).start()

    def wait_sums(h, d):
        spared = None
        if relaying(h) and d == members - 1:
            spared = my_rep == members - 1
        if relaying(h) and d == 1:
            spared = my_rep == 0
        if spared is None:
            to_member(h, d).wait_recv()
        else:
            pl.when(jnp.logical_not(spared))(lambda: to_member(h, d).wait_recv())

    def degree_to(d):
        return pltpu.make_async_remote_copy(
            src_ref=deg_send.at[d], dst_ref=deg_recv.at[d - 1],
            send_sem=d_send.at[d - 1], recv_sem=d_recv.at[d - 1],
            device_id=member_at(d), device_id_type=MESH)

    pl.semaphore_wait(barrier, len(peers))
    for o in reversed(range(1, chips)):
        to_chip(0, o).start()
    to_pair(0, 0).start()
    for copy in own_loads + [self_load, neigh_load]:
        copy.start()

    if members >= 3:
        for end, d in ((members - 1, members - 1), (0, 1)):
            @pl.when(my_rep == end)
            def _(d=d):
                for h in range(CHUNKS):
                    if relaying(h):
                        arrived[h][d - 1] = jnp.zeros_like(arrived[h][d - 1])
    weights[blocks] = jnp.zeros_like(weights[blocks])

    place_load.wait()
    count_load.wait()
    tile_load.wait()
    for o in range(1, chips):
        to_chip(0, o).wait_send()
    for h in range(1, CHUNKS):
        for o in reversed(range(1, chips)):
            to_chip(h, o).start()
        to_pair(h, 0).start()

    def place_tiles(slot):
        source = across(slot // 2, -1) * 2 + (core + slot % 2) % 2
        live = counts_ref[0, 0, source]
        spots = [
            jnp.where(k < live, places_ref[0, k, 0, source], -1) for k in range(cap)
        ]
        for q in range(members * col_tiles):
            row = ((my_rep + q // col_tiles) % members) * col_tiles + q % col_tiles
            for column in range(col_tiles):
                spot = row * col_tiles + column
                block, index = jnp.int32(blocks), jnp.int32(0)
                for k in range(cap):
                    hit = spots[k] == spot
                    block = jnp.where(hit, source, block)
                    index = jnp.where(hit, k, index)
                start = slot * own + column * tile
                if not isinstance(slot, int):
                    start = pl.multiple_of(start, tile)
                adjacency[q * tile:(q + 1) * tile, pl.ds(start, tile)] = weights[block, index]

    if blocks <= 8:
        for slot in range(blocks):
            place_tiles(slot)
    else:
        @pl.loop(0, blocks)
        def _(slot):
            place_tiles(slot)

    def forward(h):
        for o in range(1, chips):
            to_chip(h, o).wait_recv()
            to_pair(h, o).start()

    for copy in own_loads:
        copy.wait()
    forward(0)
    ones = jnp.ones((blocks * own, own), jnp.bfloat16)
    for d in range(members):
        row_sums = jnp.dot(adjacency[d * own:(d + 1) * own, :], ones,
                           preferred_element_type=jnp.float32)
        deg_send[d] = jnp.transpose(row_sums)[0:16].astype(jnp.bfloat16)
    for d in range(1, members):
        degree_to(d).start()

    group = min(members, max(1, 512 // own))
    for h in range(CHUNKS):
        if 0 < h < CHUNKS - 1:
            forward(h + 1)
        for o in range(chips):
            to_pair(h, o).wait_recv()
        size = chunk_of(width, h)[1]
        sources = gathered[h][...].reshape(blocks * own, size)
        for first in range(0, members, group):
            last = min(first + group, members)
            sums = jnp.dot(adjacency[first * own:last * own, :], sources,
                           preferred_element_type=jnp.float32).astype(jnp.bfloat16)
            partial[h][first:last] = sums.reshape(last - first, own, size)
            for d in range(max(first, 1), last):
                relay_sums(h, d)
            low = my_rep * 2 < members
            @pl.when(low)
            def _(h=h, first=first, last=last):
                for d in reversed(range(max(first, 1), last)):
                    send_sums(h, d)
            @pl.when(jnp.logical_not(low))
            def _(h=h, first=first, last=last):
                for d in range(max(first, 1), last):
                    send_sums(h, d)
        if h > 0:
            help_ends(h - 1)
        elif CHUNKS > 1:
            forward(1)

    self_load.wait()
    total[...] = jnp.dot(gathered[0][0], w_self[columns(0), :], preferred_element_type=jnp.float32)
    for h in range(1, CHUNKS):
        total[...] += jnp.dot(gathered[h][0], w_self[columns(h), :],
                              preferred_element_type=jnp.float32)
    help_ends(CHUNKS - 1)
    degree = deg_send[0].astype(jnp.float32)
    for d in range(1, members):
        degree_to(d).wait_recv()
        degree = degree + deg_recv[d - 1].astype(jnp.float32)
    inverse = jnp.transpose(jnp.broadcast_to(1.0 / (1.0 + degree[0:1]), (own, own)))[:, 0:1]
    neigh_load.wait()
    for h in range(CHUNKS):
        summed = partial[h][0].astype(jnp.float32)
        for d in range(1, members):
            wait_sums(h, d)
            summed = summed + arrived[h][d - 1].astype(jnp.float32)
        own_rows = gathered[h][0].astype(jnp.float32)
        mean = ((own_rows + summed) * inverse).astype(jnp.bfloat16)
        total[...] += jnp.dot(mean, w_neigh[columns(h), :],
                              preferred_element_type=jnp.float32)
    active = jnp.maximum(total[...], 0.0)
    scale = lax.rsqrt(jnp.mean(active * active, axis=-1, keepdims=True) + 1e-05)
    out_ref[...] = (active * scale).astype(out_ref.dtype)

    for h in range(CHUNKS):
        for o in range(1, chips):
            if h > 0:
                to_chip(h, o).wait_send()
        for o in range(chips):
            to_pair(h, o).wait_send()
        for d in range(1, members):
            to_member(h, d).wait_send()
    for d in range(1, members):
        degree_to(d).wait_send()


def on_device(stale, w_self, w_neigh, tile_weights, tile_pos, tile_counts):
    blocks = lax.axis_size("blk")
    members = lax.axis_size("rep")
    own, width = stale.shape
    cap, tile = tile_weights.shape[3], tile_weights.shape[4]
    chips = blocks // 2
    sizes = [chunk_of(width, h)[1] for h in range(CHUNKS)]
    def buffers(count):
        return tuple(pltpu.VMEM((count, own, size), bf16) for size in sizes)
    bf16, f32 = jnp.bfloat16, jnp.float32
    dma = pltpu.SemaphoreType.DMA
    vmem = pl.BlockSpec(memory_space=pltpu.VMEM)
    hbm = pl.BlockSpec(memory_space=pl.ANY)
    flops = 2 * own * width * (members * own * blocks + 2 * width)
    return pl.pallas_call(
        functools.partial(refresh_kernel, blocks, members),
        out_shape=pltpu.VMEM((own, width), bf16),
        in_specs=[hbm] * 6,
        out_specs=vmem,
        scratch_shapes=[
            pltpu.SMEM((1, cap, 1, blocks), jnp.int32),
            pltpu.SMEM((1, 1, blocks), jnp.int32),
            pltpu.VMEM(w_self.shape, bf16),
            pltpu.VMEM(w_neigh.shape, bf16),
            pltpu.VMEM((blocks + 1, cap, tile, tile), bf16),
            pltpu.VMEM((members * own, blocks * own), bf16),
            buffers(blocks),
            buffers(members),
            buffers(members - 1),
            pltpu.VMEM((members, 16, own), bf16),
            pltpu.VMEM((members - 1, 16, own), bf16),
            buffers(2),
            pltpu.VMEM((own, width), f32),
            dma((CHUNKS + 5,)),
            dma((CHUNKS, chips)),
            dma((CHUNKS, chips)),
            dma((CHUNKS, chips)),
            dma((CHUNKS, chips)),
            dma((CHUNKS, members - 1)),
            dma((CHUNKS, members - 1)),
            dma((members - 1,)),
            dma((members - 1,)),
            dma((2, CHUNKS)),
        ],
        compiler_params=pltpu.CompilerParams(
            collective_id=0, has_side_effects=True, vmem_limit_bytes=60 * 1024 * 1024),
        cost_estimate=pl.CostEstimate(
            flops=flops, bytes_accessed=2 * (tile_weights.size + 4 * own * width), transcendentals=own),
        name="refresh",
    )(stale, w_self, w_neigh, tile_weights, jnp.transpose(tile_pos, (0, 3, 1, 2)), tile_counts)


def solution(mesh):
    return jax.shard_map(
        on_device,
        mesh=mesh,
        in_specs=(
            P(("blk", "rep"), None),
            P(),
            P(),
            P("blk", "rep", None, None, None, None),
            P("blk", "rep", None, None),
            P("blk", "rep", None),
        ),
        out_specs=P(("blk", "rep"), None),
        check_vma=False,
    )
```

```python
import functools

import jax
import jax.numpy as jnp
from jax import lax
from jax.experimental import pallas as pl
from jax.experimental.pallas import tpu as pltpu
from jax.sharding import PartitionSpec as P

MESH = pl.DeviceIdType.MESH
QUARTERS = (1, 1, 1, 1)
CHUNKS = len(QUARTERS)


def chunk_of(width, h):
    unit = width // sum(QUARTERS)
    return sum(QUARTERS[:h]) * unit, QUARTERS[h] * unit


def refresh_kernel(
    blocks, members, stale_hbm, w_self_hbm, w_neigh_hbm, weights_hbm, places_hbm, counts_hbm,
    out_ref,
    places_ref, counts_ref, w_self, w_neigh, weights, adjacency, gathered, partial, arrived, deg_send, deg_recv, relayed, total,
    load_sem, g_send, g_recv, f_send, f_recv, p_send, p_recv, d_send, d_recv, r_recv,
):
    own, width = stale_hbm.shape
    cap, tile = weights_hbm.shape[3], weights_hbm.shape[4]
    col_tiles = own // tile
    chips = blocks // 2
    my_blk = lax.axis_index("blk")
    my_rep = lax.axis_index("rep")
    chip, core = my_blk // 2, my_blk % 2

    def columns(h):
        return pl.ds(*chunk_of(width, h))

    def load(slot, source, target):
        return pltpu.make_async_copy(source, target, load_sem.at[slot])

    own_loads = [
        load(h, stale_hbm.at[:, columns(h)], gathered[h].at[0])
        for h in range(CHUNKS)
    ]
    place_load = load(CHUNKS, places_hbm, places_ref)
    count_load = load(CHUNKS + 1, counts_hbm, counts_ref)
    tile_load = load(CHUNKS + 2, weights_hbm.at[0, 0], weights.at[pl.ds(0, blocks)])
    self_load = load(CHUNKS + 3, w_self_hbm, w_self)
    neigh_load = load(CHUNKS + 4, w_neigh_hbm, w_neigh)

    pair = {"blk": chip * 2 + 1 - core}
    def across(offset, sign):
        if chips & (chips - 1):
            return (chip + chips + sign * offset) % chips
        other, bit = 0, 1
        while bit < chips:
            other = other + (chip // bit % 2 + offset // bit % 2) % 2 * bit
            bit *= 2
        return other
    def chip_at(offset):
        return {"blk": across(offset, 1) * 2 + core}
    def member_at(offset):
        return {"rep": (my_rep + offset) % members}

    barrier = pltpu.get_barrier_semaphore()
    peers = [member_at(d) for d in range(1, members)]
    peers += [chip_at(o) for o in range(1, chips)] + [pair]
    for peer in peers:
        pl.semaphore_signal(barrier, inc=1, device_id=peer, device_id_type=MESH)
    for copy in [place_load, count_load, tile_load]:
        copy.start()

    def to_chip(h, o):
        return pltpu.make_async_remote_copy(
            src_ref=stale_hbm.at[:, columns(h)] if h == 0 else gathered[h].at[0],
            dst_ref=gathered[h].at[2 * o],
            send_sem=g_send.at[h, o], recv_sem=g_recv.at[h, o],
            device_id=chip_at(o), device_id_type=MESH)

    def to_pair(h, o):
        source = stale_hbm.at[:, columns(h)] if h + o == 0 else gathered[h].at[2 * o]
        return pltpu.make_async_remote_copy(
            src_ref=source, dst_ref=gathered[h].at[2 * o + 1],
            send_sem=f_send.at[h, o], recv_sem=f_recv.at[h, o],
            device_id=pair, device_id_type=MESH)

    def to_member(h, d):
        return pltpu.make_async_remote_copy(
            src_ref=partial[h].at[d], dst_ref=arrived[h].at[d - 1],
            send_sem=p_send.at[h, d - 1], recv_sem=p_recv.at[h, d - 1],
            device_id=member_at(d), device_id_type=MESH)

    def relaying(h):
        return members >= 3 and h < CHUNKS - 1
    def to_relay(h, side):
        d, helper = (members - 1, 1) if side == 0 else (1, members - 2)
        return pltpu.make_async_remote_copy(
            src_ref=partial[h].at[d], dst_ref=relayed[h].at[side],
            send_sem=p_send.at[h, d - 1], recv_sem=r_recv.at[side, h],
            device_id={"rep": helper}, device_id_type=MESH)

    def ends_at(h, d):
        found = []
        if relaying(h) and d == members - 1:
            found.append((0, my_rep == 0))
        if relaying(h) and d == 1:
            found.append((1, my_rep == members - 1))
        return found

    def helps_at(h, d):
        found = []
        if relaying(h) and d == members - 2:
            found.append((0, my_rep == 1))
        if relaying(h) and d == 2:
            found.append((1, my_rep == members - 2))
        return found

    def relay_sums(h, d):
        for side, here in ends_at(h, d):
            pl.when(here)(lambda side=side: to_relay(h, side).start())

    def send_sums(h, d):
        direct = None
        for side, here in ends_at(h, d) + helps_at(h, d):
            direct = jnp.logical_not(here) if direct is None else direct & jnp.logical_not(here)
        if direct is None:
            to_member(h, d).start()
        else:
            pl.when(direct)(lambda: to_member(h, d).start())

    def help_ends(h):
        for d in range(1, members):
            for side, here in helps_at(h, d):
                @pl.when(here)
                def _(d=d, side=side):
                    to_relay(h, side).wait_recv()
                    both = partial[h][d].astype(jnp.float32) + relayed[h][side].astype(jnp.float32)
                    partial[h][d] = both.astype(jnp.bfloat16)
                    to_member(h, d).start()

    def wait_sums(h, d):
        spared = None
        if relaying(h) and d == members - 1:
            spared = my_rep == members - 1
        if relaying(h) and d == 1:
            spared = my_rep == 0
        if spared is None:
            to_member(h, d).wait_recv()
        else:
            pl.when(jnp.logical_not(spared))(lambda: to_member(h, d).wait_recv())

    def degree_to(d):
        return pltpu.make_async_remote_copy(
            src_ref=deg_send.at[d], dst_ref=deg_recv.at[d - 1],
            send_sem=d_send.at[d - 1], recv_sem=d_recv.at[d - 1],
            device_id=member_at(d), device_id_type=MESH)

    pl.semaphore_wait(barrier, len(peers))
    for o in reversed(range(1, chips)):
        to_chip(0, o).start()
    to_pair(0, 0).start()
    for copy in own_loads + [self_load, neigh_load]:
        copy.start()

    if members >= 3:
        for end, d in ((members - 1, members - 1), (0, 1)):
            @pl.when(my_rep == end)
            def _(d=d):
                for h in range(CHUNKS):
                    if relaying(h):
                        arrived[h][d - 1] = jnp.zeros_like(arrived[h][d - 1])
    weights[blocks] = jnp.zeros_like(weights[blocks])

    place_load.wait()
    count_load.wait()
    tile_load.wait()
    for o in range(1, chips):
        to_chip(0, o).wait_send()
    for copy in own_loads:
        copy.wait()
    def spread(h):
        for o in reversed(range(1, chips)):
            to_chip(h, o).start()
        to_pair(h, 0).start()

    spread(1)

    def place_tiles(slot):
        source = across(slot // 2, -1) * 2 + (core + slot % 2) % 2
        live = counts_ref[0, 0, source]
        spots = [
            jnp.where(k < live, places_ref[0, k, 0, source], -1) for k in range(cap)
        ]
        for q in range(members * col_tiles):
            row = ((my_rep + q // col_tiles) % members) * col_tiles + q % col_tiles
            for column in range(col_tiles):
                spot = row * col_tiles + column
                block, index = jnp.int32(blocks), jnp.int32(0)
                for k in range(cap):
                    hit = spots[k] == spot
                    block = jnp.where(hit, source, block)
                    index = jnp.where(hit, k, index)
                start = slot * own + column * tile
                if not isinstance(slot, int):
                    start = pl.multiple_of(start, tile)
                adjacency[q * tile:(q + 1) * tile, pl.ds(start, tile)] = weights[block, index]

    if blocks <= 8:
        for slot in range(blocks):
            place_tiles(slot)
    else:
        @pl.loop(0, blocks)
        def _(slot):
            place_tiles(slot)

    def forward(h):
        for o in range(1, chips):
            to_chip(h, o).wait_recv()
            to_pair(h, o).start()

    spread(2)
    forward(0)
    for h in range(3, CHUNKS):
        spread(h)
    ones = jnp.ones((blocks * own, own), jnp.bfloat16)
    for d in range(members):
        row_sums = jnp.dot(adjacency[d * own:(d + 1) * own, :], ones,
                           preferred_element_type=jnp.float32)
        deg_send[d] = jnp.transpose(row_sums)[0:16].astype(jnp.bfloat16)
    for d in range(1, members):
        degree_to(d).start()

    group = min(members, max(1, 512 // own))
    for h in range(CHUNKS):
        if 0 < h < CHUNKS - 1:
            forward(h + 1)
        for o in range(chips):
            to_pair(h, o).wait_recv()
        size = chunk_of(width, h)[1]
        sources = gathered[h][...].reshape(blocks * own, size)
        for first in range(0, members, group):
            last = min(first + group, members)
            sums = jnp.dot(adjacency[first * own:last * own, :], sources,
                           preferred_element_type=jnp.float32).astype(jnp.bfloat16)
            partial[h][first:last] = sums.reshape(last - first, own, size)
            for d in range(max(first, 1), last):
                relay_sums(h, d)
            low = my_rep * 2 < members
            @pl.when(low)
            def _(h=h, first=first, last=last):
                for d in reversed(range(max(first, 1), last)):
                    send_sums(h, d)
            @pl.when(jnp.logical_not(low))
            def _(h=h, first=first, last=last):
                for d in range(max(first, 1), last):
                    send_sums(h, d)
        if h > 0:
            help_ends(h - 1)
        elif CHUNKS > 1:
            forward(1)

    self_load.wait()
    total[...] = jnp.dot(gathered[0][0], w_self[columns(0), :], preferred_element_type=jnp.float32)
    for h in range(1, CHUNKS):
        total[...] += jnp.dot(gathered[h][0], w_self[columns(h), :],
                              preferred_element_type=jnp.float32)
    help_ends(CHUNKS - 1)
    degree = deg_send[0].astype(jnp.float32)
    for d in range(1, members):
        degree_to(d).wait_recv()
        degree = degree + deg_recv[d - 1].astype(jnp.float32)
    inverse = jnp.transpose(jnp.broadcast_to(1.0 / (1.0 + degree[0:1]), (own, own)))[:, 0:1]
    neigh_load.wait()
    for h in range(CHUNKS):
        summed = partial[h][0].astype(jnp.float32)
        for d in range(1, members):
            wait_sums(h, d)
            summed = summed + arrived[h][d - 1].astype(jnp.float32)
        own_rows = gathered[h][0].astype(jnp.float32)
        mean = ((own_rows + summed) * inverse).astype(jnp.bfloat16)
        total[...] += jnp.dot(mean, w_neigh[columns(h), :],
                              preferred_element_type=jnp.float32)
    active = jnp.maximum(total[...], 0.0)
    scale = lax.rsqrt(jnp.mean(active * active, axis=-1, keepdims=True) + 1e-05)
    out_ref[...] = (active * scale).astype(out_ref.dtype)

    for h in range(CHUNKS):
        for o in range(1, chips):
            if h > 0:
                to_chip(h, o).wait_send()
        for o in range(chips):
            to_pair(h, o).wait_send()
        for d in range(1, members):
            to_member(h, d).wait_send()
    for d in range(1, members):
        degree_to(d).wait_send()


def on_device(stale, w_self, w_neigh, tile_weights, tile_pos, tile_counts):
    blocks = lax.axis_size("blk")
    members = lax.axis_size("rep")
    own, width = stale.shape
    cap, tile = tile_weights.shape[3], tile_weights.shape[4]
    chips = blocks // 2
    sizes = [chunk_of(width, h)[1] for h in range(CHUNKS)]
    def buffers(count):
        return tuple(pltpu.VMEM((count, own, size), bf16) for size in sizes)
    bf16, f32 = jnp.bfloat16, jnp.float32
    dma = pltpu.SemaphoreType.DMA
    vmem = pl.BlockSpec(memory_space=pltpu.VMEM)
    hbm = pl.BlockSpec(memory_space=pl.ANY)
    flops = 2 * own * width * (members * own * blocks + 2 * width)
    return pl.pallas_call(
        functools.partial(refresh_kernel, blocks, members),
        out_shape=pltpu.VMEM((own, width), bf16),
        in_specs=[hbm] * 6,
        out_specs=vmem,
        scratch_shapes=[
            pltpu.SMEM((1, cap, 1, blocks), jnp.int32),
            pltpu.SMEM((1, 1, blocks), jnp.int32),
            pltpu.VMEM(w_self.shape, bf16),
            pltpu.VMEM(w_neigh.shape, bf16),
            pltpu.VMEM((blocks + 1, cap, tile, tile), bf16),
            pltpu.VMEM((members * own, blocks * own), bf16),
            buffers(blocks),
            buffers(members),
            buffers(members - 1),
            pltpu.VMEM((members, 16, own), bf16),
            pltpu.VMEM((members - 1, 16, own), bf16),
            buffers(2),
            pltpu.VMEM((own, width), f32),
            dma((CHUNKS + 5,)),
            dma((CHUNKS, chips)),
            dma((CHUNKS, chips)),
            dma((CHUNKS, chips)),
            dma((CHUNKS, chips)),
            dma((CHUNKS, members - 1)),
            dma((CHUNKS, members - 1)),
            dma((members - 1,)),
            dma((members - 1,)),
            dma((2, CHUNKS)),
        ],
        compiler_params=pltpu.CompilerParams(
            collective_id=0, has_side_effects=True, vmem_limit_bytes=60 * 1024 * 1024),
        cost_estimate=pl.CostEstimate(
            flops=flops, bytes_accessed=2 * (tile_weights.size + 4 * own * width), transcendentals=own),
        name="refresh",
    )(stale, w_self, w_neigh, tile_weights, jnp.transpose(tile_pos, (0, 3, 1, 2)), tile_counts)


def solution(mesh):
    return jax.shard_map(
        on_device,
        mesh=mesh,
        in_specs=(
            P(("blk", "rep"), None),
            P(),
            P(),
            P("blk", "rep", None, None, None, None),
            P("blk", "rep", None, None),
            P("blk", "rep", None),
        ),
        out_specs=P(("blk", "rep"), None),
        check_vma=False,
    )
```

```python
import functools

import jax
import jax.numpy as jnp
from jax import lax
from jax.experimental import pallas as pl
from jax.experimental.pallas import tpu as pltpu
from jax.sharding import PartitionSpec as P

MESH = pl.DeviceIdType.MESH
CHUNKS = 4


def refresh_kernel(
    blocks, members, stale_hbm, w_self_hbm, w_neigh_hbm, weights_hbm, places_hbm, counts_hbm,
    out_ref,
    places_ref, counts_ref, w_self, w_neigh, weights, adjacency, gathered, partial, arrived, deg_send, deg_recv, relayed, total,
    load_sem, g_send, g_recv, f_send, f_recv, p_send, p_recv, d_send, d_recv, r_recv,
):
    own, width = stale_hbm.shape
    cap, tile = weights_hbm.shape[3], weights_hbm.shape[4]
    col_tiles = own // tile
    chips = blocks // 2
    chunk = width // CHUNKS
    my_blk = lax.axis_index("blk")
    my_rep = lax.axis_index("rep")
    chip, core = my_blk // 2, my_blk % 2

    def load(slot, source, target):
        return pltpu.make_async_copy(source, target, load_sem.at[slot])

    own_loads = [
        load(h, stale_hbm.at[:, pl.ds(h * chunk, chunk)], gathered.at[h, 0])
        for h in range(CHUNKS)
    ]
    place_load = load(CHUNKS, places_hbm, places_ref)
    count_load = load(CHUNKS + 1, counts_hbm, counts_ref)
    tile_load = load(CHUNKS + 2, weights_hbm.at[0, 0], weights.at[pl.ds(0, blocks)])
    self_load = load(CHUNKS + 3, w_self_hbm, w_self)
    neigh_load = load(CHUNKS + 4, w_neigh_hbm, w_neigh)

    pair = {"blk": chip * 2 + 1 - core}
    def across(offset, sign):
        if chips & (chips - 1):
            return (chip + chips + sign * offset) % chips
        other, bit = 0, 1
        while bit < chips:
            other = other + (chip // bit % 2 + offset // bit % 2) % 2 * bit
            bit *= 2
        return other
    def chip_at(offset):
        return {"blk": across(offset, 1) * 2 + core}
    def member_at(offset):
        return {"rep": (my_rep + offset) % members}

    barrier = pltpu.get_barrier_semaphore()
    peers = [member_at(d) for d in range(1, members)]
    peers += [chip_at(o) for o in range(1, chips)] + [pair]
    for peer in peers:
        pl.semaphore_signal(barrier, inc=1, device_id=peer, device_id_type=MESH)
    for copy in [place_load, count_load, tile_load]:
        copy.start()

    def to_chip(h, o):
        return pltpu.make_async_remote_copy(
            src_ref=stale_hbm.at[:, pl.ds(h * chunk, chunk)], dst_ref=gathered.at[h, 2 * o],
            send_sem=g_send.at[h, o], recv_sem=g_recv.at[h, o],
            device_id=chip_at(o), device_id_type=MESH)

    def to_pair(h, o):
        source = stale_hbm.at[:, pl.ds(h * chunk, chunk)] if o == 0 else gathered.at[h, 2 * o]
        return pltpu.make_async_remote_copy(
            src_ref=source, dst_ref=gathered.at[h, 2 * o + 1],
            send_sem=f_send.at[h, o], recv_sem=f_recv.at[h, o],
            device_id=pair, device_id_type=MESH)

    def to_member(h, d):
        return pltpu.make_async_remote_copy(
            src_ref=partial.at[h, d], dst_ref=arrived.at[h, d - 1],
            send_sem=p_send.at[h, d - 1], recv_sem=p_recv.at[h, d - 1],
            device_id=member_at(d), device_id_type=MESH)

    def relaying(h):
        return members >= 3 and h < CHUNKS // 2
    def to_relay(h, side):
        d, helper = (members - 1, 1) if side == 0 else (1, members - 2)
        return pltpu.make_async_remote_copy(
            src_ref=partial.at[h, d], dst_ref=relayed.at[side, h],
            send_sem=p_send.at[h, d - 1], recv_sem=r_recv.at[side, h],
            device_id={"rep": helper}, device_id_type=MESH)

    def ends_at(h, d):
        found = []
        if relaying(h) and d == members - 1:
            found.append((0, my_rep == 0))
        if relaying(h) and d == 1:
            found.append((1, my_rep == members - 1))
        return found

    def helps_at(h, d):
        found = []
        if relaying(h) and d == members - 2:
            found.append((0, my_rep == 1))
        if relaying(h) and d == 2:
            found.append((1, my_rep == members - 2))
        return found

    def relay_sums(h, d):
        for side, here in ends_at(h, d):
            pl.when(here)(lambda side=side: to_relay(h, side).start())

    def send_sums(h, d):
        direct = None
        for side, here in ends_at(h, d) + helps_at(h, d):
            direct = jnp.logical_not(here) if direct is None else direct & jnp.logical_not(here)
        if direct is None:
            to_member(h, d).start()
        else:
            pl.when(direct)(lambda: to_member(h, d).start())

    def help_ends(h):
        for d in range(1, members):
            for side, here in helps_at(h, d):
                @pl.when(here)
                def _(d=d, side=side):
                    to_relay(h, side).wait_recv()
                    both = partial[h, d].astype(jnp.float32) + relayed[side, h].astype(jnp.float32)
                    partial[h, d] = both.astype(jnp.bfloat16)
                    to_member(h, d).start()

    def wait_sums(h, d):
        spared = None
        if relaying(h) and d == members - 1:
            spared = my_rep == members - 1
        if relaying(h) and d == 1:
            spared = my_rep == 0
        if spared is None:
            to_member(h, d).wait_recv()
        else:
            pl.when(jnp.logical_not(spared))(lambda: to_member(h, d).wait_recv())

    def degree_to(d):
        return pltpu.make_async_remote_copy(
            src_ref=deg_send.at[d], dst_ref=deg_recv.at[d - 1],
            send_sem=d_send.at[d - 1], recv_sem=d_recv.at[d - 1],
            device_id=member_at(d), device_id_type=MESH)

    pl.semaphore_wait(barrier, len(peers))
    for o in reversed(range(1, chips)):
        to_chip(0, o).start()
    to_pair(0, 0).start()
    for copy in own_loads + [self_load, neigh_load]:
        copy.start()

    if members >= 3:
        for end, d in ((members - 1, members - 1), (0, 1)):
            @pl.when(my_rep == end)
            def _(d=d):
                for h in range(CHUNKS):
                    if relaying(h):
                        arrived[h, d - 1] = jnp.zeros_like(arrived[h, d - 1])
    weights[blocks] = jnp.zeros_like(weights[blocks])

    place_load.wait()
    count_load.wait()
    tile_load.wait()
    def place_tiles(slot):
        source = across(slot // 2, -1) * 2 + (core + slot % 2) % 2
        live = counts_ref[0, 0, source]
        spots = [
            jnp.where(k < live, places_ref[0, k, 0, source], -1) for k in range(cap)
        ]
        for q in range(members * col_tiles):
            row = ((my_rep + q // col_tiles) % members) * col_tiles + q % col_tiles
            for column in range(col_tiles):
                spot = row * col_tiles + column
                block, index = jnp.int32(blocks), jnp.int32(0)
                for k in range(cap):
                    hit = spots[k] == spot
                    block = jnp.where(hit, source, block)
                    index = jnp.where(hit, k, index)
                start = slot * own + column * tile
                if not isinstance(slot, int):
                    start = pl.multiple_of(start, tile)
                adjacency[q * tile:(q + 1) * tile, pl.ds(start, tile)] = weights[block, index]

    if blocks <= 8:
        for slot in range(blocks):
            place_tiles(slot)
    else:
        @pl.loop(0, blocks)
        def _(slot):
            place_tiles(slot)

    ones = jnp.ones((blocks * own, own), jnp.bfloat16)
    for d in range(members):
        row_sums = jnp.dot(adjacency[d * own:(d + 1) * own, :], ones,
                           preferred_element_type=jnp.float32)
        deg_send[d] = jnp.transpose(row_sums)[0:16].astype(jnp.bfloat16)
    for d in range(1, members):
        degree_to(d).start()

    for o in range(1, chips):
        to_chip(0, o).wait_send()
    for h in range(1, CHUNKS):
        for o in reversed(range(1, chips)):
            to_chip(h, o).start()
        to_pair(h, 0).start()

    def forward(h):
        for o in range(1, chips):
            to_chip(h, o).wait_recv()
            to_pair(h, o).start()

    for copy in own_loads:
        copy.wait()
    forward(0)
    group = min(members, max(1, 512 // own))
    for h in range(CHUNKS):
        if 0 < h < CHUNKS - 1:
            forward(h + 1)
        for o in range(chips):
            to_pair(h, o).wait_recv()
        sources = gathered[h].reshape(blocks * own, chunk)
        for first in range(0, members, group):
            last = min(first + group, members)
            sums = jnp.dot(adjacency[first * own:last * own, :], sources,
                           preferred_element_type=jnp.float32).astype(jnp.bfloat16)
            partial[h, first:last] = sums.reshape(last - first, own, chunk)
            for d in range(max(first, 1), last):
                relay_sums(h, d)
            low = my_rep * 2 < members
            @pl.when(low)
            def _(h=h, first=first, last=last):
                for d in reversed(range(max(first, 1), last)):
                    send_sums(h, d)
            @pl.when(jnp.logical_not(low))
            def _(h=h, first=first, last=last):
                for d in range(max(first, 1), last):
                    send_sums(h, d)
        if h > 0:
            help_ends(h - 1)
        elif CHUNKS > 1:
            forward(1)

    self_load.wait()
    total[...] = jnp.dot(gathered[0, 0], w_self[0:chunk, :], preferred_element_type=jnp.float32)
    for h in range(1, CHUNKS):
        total[...] += jnp.dot(gathered[h, 0], w_self[h * chunk:(h + 1) * chunk, :],
                              preferred_element_type=jnp.float32)
    help_ends(CHUNKS - 1)
    degree = deg_send[0].astype(jnp.float32)
    for d in range(1, members):
        degree_to(d).wait_recv()
        degree = degree + deg_recv[d - 1].astype(jnp.float32)
    inverse = jnp.transpose(jnp.broadcast_to(1.0 / (1.0 + degree[0:1]), (own, own)))[:, 0:1]
    neigh_load.wait()
    for h in range(CHUNKS):
        summed = partial[h, 0].astype(jnp.float32)
        for d in range(1, members):
            wait_sums(h, d)
            summed = summed + arrived[h, d - 1].astype(jnp.float32)
        own_rows = gathered[h, 0].astype(jnp.float32)
        mean = ((own_rows + summed) * inverse).astype(jnp.bfloat16)
        total[...] += jnp.dot(mean, w_neigh[h * chunk:(h + 1) * chunk, :],
                              preferred_element_type=jnp.float32)
    active = jnp.maximum(total[...], 0.0)
    scale = lax.rsqrt(jnp.mean(active * active, axis=-1, keepdims=True) + 1e-05)
    out_ref[...] = (active * scale).astype(out_ref.dtype)

    for h in range(CHUNKS):
        for o in range(1, chips):
            if h > 0:
                to_chip(h, o).wait_send()
        for o in range(chips):
            to_pair(h, o).wait_send()
        for d in range(1, members):
            to_member(h, d).wait_send()
    for d in range(1, members):
        degree_to(d).wait_send()


def on_device(stale, w_self, w_neigh, tile_weights, tile_pos, tile_counts):
    blocks = lax.axis_size("blk")
    members = lax.axis_size("rep")
    own, width = stale.shape
    cap, tile = tile_weights.shape[3], tile_weights.shape[4]
    chips = blocks // 2
    chunk = width // CHUNKS
    bf16, f32 = jnp.bfloat16, jnp.float32
    dma = pltpu.SemaphoreType.DMA
    vmem = pl.BlockSpec(memory_space=pltpu.VMEM)
    hbm = pl.BlockSpec(memory_space=pl.ANY)
    flops = 2 * own * width * (members * own * blocks + 2 * width)
    return pl.pallas_call(
        functools.partial(refresh_kernel, blocks, members),
        out_shape=pltpu.VMEM((own, width), bf16),
        in_specs=[hbm] * 6,
        out_specs=vmem,
        scratch_shapes=[
            pltpu.SMEM((1, cap, 1, blocks), jnp.int32),
            pltpu.SMEM((1, 1, blocks), jnp.int32),
            pltpu.VMEM(w_self.shape, bf16),
            pltpu.VMEM(w_neigh.shape, bf16),
            pltpu.VMEM((blocks + 1, cap, tile, tile), bf16),
            pltpu.VMEM((members * own, blocks * own), bf16),
            pltpu.VMEM((CHUNKS, blocks, own, chunk), bf16),
            pltpu.VMEM((CHUNKS, members, own, chunk), bf16),
            pltpu.VMEM((CHUNKS, members - 1, own, chunk), bf16),
            pltpu.VMEM((members, 16, own), bf16),
            pltpu.VMEM((members - 1, 16, own), bf16),
            pltpu.VMEM((2, CHUNKS, own, chunk), bf16),
            pltpu.VMEM((own, width), f32),
            dma((CHUNKS + 5,)),
            dma((CHUNKS, chips)),
            dma((CHUNKS, chips)),
            dma((CHUNKS, chips)),
            dma((CHUNKS, chips)),
            dma((CHUNKS, members - 1)),
            dma((CHUNKS, members - 1)),
            dma((members - 1,)),
            dma((members - 1,)),
            dma((2, CHUNKS)),
        ],
        compiler_params=pltpu.CompilerParams(
            collective_id=0, has_side_effects=True, vmem_limit_bytes=60 * 1024 * 1024),
        cost_estimate=pl.CostEstimate(
            flops=flops, bytes_accessed=2 * (tile_weights.size + 4 * own * width), transcendentals=own),
        name="refresh",
    )(stale, w_self, w_neigh, tile_weights, jnp.transpose(tile_pos, (0, 3, 1, 2)), tile_counts)


def solution(mesh):
    return jax.shard_map(
        on_device,
        mesh=mesh,
        in_specs=(
            P(("blk", "rep"), None),
            P(),
            P(),
            P("blk", "rep", None, None, None, None),
            P("blk", "rep", None, None),
            P("blk", "rep", None),
        ),
        out_specs=P(("blk", "rep"), None),
        check_vma=False,
    )
```
